32 devices in a mesh: groups: 2 (over x), loop: 4 (over y, core), cuts: 4 (over z).
Axes of the slice: x: 2, y: 2, z: 4, core: 2. Of those that a mesh axis runs over, the one named last changes fastest.
Arguments:
- vectors: bfloat16 [128, 64, 256], P(('groups', 'loop'), 'cuts'), parts along dimension 0, may hold values from -6 to 6
- near_tiles: bfloat16 [384, 256, 256], P(('groups', 'loop')), parts along dimension 0, may hold values from -0.1875 to 0.1875
- self_tiles: bfloat16 [128, 256, 256], P(('groups', 'loop')), parts along dimension 0, may hold values from -0.1875 to 0.1875
- source_home: int32 [384, 1], P(('groups', 'loop')), parts along dimension 0, may hold values from 0 to 3; in each aligned block of 48 rows (0 to 47, 48 to 95, ...) at most 24 rows name the same one
- target_home: int32 [384, 1], P(('groups', 'loop')), parts along dimension 0, may hold values from 0 to 3; in each aligned block of 48 rows (0 to 47, 48 to 95, ...) at most 24 rows name the same one
- block_local: int32 [384, 2], P(('groups', 'loop')), parts along dimension 0, may hold values from 0 to 15
- column_basis: bfloat16 [128, 64, 256], P(('groups', 'loop')), parts along dimension 0, may hold values from -0.375 to 0.375
- row_basis: bfloat16 [128, 64, 256], P(('groups', 'loop')), parts along dimension 0, may hold values from -0.375 to 0.375
- column_transfer: bfloat16 [128, 64, 64], P(('groups', 'loop')), parts along dimension 0, may hold values from -0.5 to 0.5
- row_transfer: bfloat16 [128, 64, 64], P(('groups', 'loop')), parts along dimension 0, may hold values from -0.75 to 0.75
- coupling: bfloat16 [64, 64, 512], P(('groups', 'loop')), parts along dimension 0, may hold values from -0.25 to 0.25
- far_source: int32 [64, 8], P(('groups', 'loop')), parts along dimension 0, may hold values from 0 to 31
Outputs:
- product: bfloat16 [128, 64, 256], P(('groups', 'loop'), 'cuts'), parts along dimension 0
The draws below stay inside these ranges and needn't reach their ends.
There are 2 independent parts, one for each index of `groups`. The reference program is written for one: setup_inputs(seed, part) draws one part's arguments, and reference() takes and returns one part's arrays. A program takes and returns all parts, laid end to end along the dimension named above; each array names one. Nothing has to cross between parts.
Inputs may be any that keep to these rules, and one draw needn't show every extreme that they name: `source_home`: among the 48 blocks of one index of loop, no value is named by more than 24 of them, and in every draw some value is named by exactly 24 of them on some index. `target_home`: among the 48 blocks of one index of loop, no value is named by more than 24 of them, and in every draw some value is named by exactly 24 of them on some index.
All inputs are finite; a program needn't handle non-finite values.
Results may differ from the reference program's by a relative error of at most 0.0058.
Values may be sent and summed in bfloat16 or wider, within the bound.
No kernel may reach another device: no remote copies, remote signals or barrier semaphores. Data moves between devices by JAX's collectives and lax.ppermute only.
A program may use at most 64 MiB of HBM per device.

```python
import math
import jax
import jax.numpy as jnp
import numpy as np
from jax import lax

LEAF = 256
RANK = 64
NV = 64
ITERS = 2
CL = 16
FAR = 8
BLK = 48
SLOT = 24
NC = 64
NP = 32
NB = 192
N_LOOP = 4


def with_ends(array, key, low, top_value):
    longest = array.shape.index(max(array.shape))
    spots = []
    for shift in (0, 1):
        where = [jax.random.randint(jax.random.fold_in(key, axis), (), 0, length) for axis, length in enumerate(array.shape)]
        where[longest] = (where[longest] + shift) % array.shape[longest]
        spots.append(tuple(where))
    return array.at[spots[0]].set(low).at[spots[1]].set(top_value)


def block_scale(own_key, dims, cuts, smallest, top_value):
    def one(position, shards_of):
        draws = jax.random.uniform(jax.random.fold_in(jax.random.fold_in(own_key, 6), position), (shards_of,), jnp.float32, smallest / len(cuts), top_value / len(cuts))
        return jnp.repeat(jnp.exp(draws), dims[position] // shards_of).reshape((-1,) + (1,) * (len(dims) - position - 1))

    factor_of = one(*cuts[0])
    for cut in cuts[1:]:
        factor_of = factor_of * one(*cut)
    return factor_of


def routed_block(stream_key, own, number, rows, amount, top, most, lean):
    ranking = jax.random.permutation(stream_key, amount)
    packed, ordinary = shares(amount, rows * top, most, lean, True), shares(amount, rows * top, most, lean, False)
    places = jnp.arange(amount)

    def named(sizes, turn):
        used = int((sizes > 0).sum())
        fixed = max(1, used // 4)
        shifted = fixed + (places - fixed + turn * (used - fixed)) % max(1, amount - fixed)
        return jnp.zeros((amount,), jnp.int32).at[ranking[jnp.where(places < fixed, places, shifted)]].set(jnp.asarray(sizes, jnp.int32))

    sizes = jnp.where(number % 4 == 0, named(packed, number // 4), named(ordinary, number - number // 4 - 1))
    mixed = jax.random.permutation(jax.random.fold_in(own, 3), amount)
    source_of, sink = mixed[0:amount // 2 * 2:2], mixed[1:amount // 2 * 2:2]
    slack = jnp.minimum(sizes[source_of] - 1, most - sizes[sink]) // 2
    slack = jnp.where((source_of == ranking[0]) | (sink == ranking[0]) | (sizes[sink] == 0), 0, jnp.maximum(slack, 0))
    shifted = jax.random.randint(jax.random.fold_in(own, 4), (amount // 2,), 0, 1 << 20) % (slack + 1)
    sizes = sizes.at[source_of].add(-shifted).at[sink].add(shifted)
    items = jnp.searchsorted(jnp.cumsum(sizes), jnp.arange(rows * top), side="right").astype(jnp.int32)
    table = items.reshape(top, rows).T
    table = table[jax.random.permutation(jax.random.fold_in(own, 1), rows)]
    turn = jax.random.randint(jax.random.fold_in(own, 2), (rows, 1), 0, top)
    return jnp.take_along_axis(table, (jnp.arange(top)[None, :] + turn) % top, axis=1)


def shares(number_of, total, most, lean, full):
    weights = [(1 << 20) // math.isqrt(standing ** lean) + 1 for standing in range(1, number_of + 1)]
    largest = most if full else min(most, max(-(-total // number_of), total * weights[0] // sum(weights)))
    least = 1 if total - largest >= number_of - 1 else 0
    holding, rest = [largest] + [least] * (number_of - 1), total - largest - least * (number_of - 1)
    while rest > 0:
        movable = [i for i in range(1, number_of) if holding[i] < largest] or [i for i in range(1, number_of) if holding[i] < most]
        whole, remaining = sum([weights[i] for i in movable]), rest
        for i in movable:
            addition = min(most - holding[i], max(1, remaining * weights[i] // whole), rest)
            holding[i] = holding[i] + addition
            rest = rest - addition
    return np.array(holding)


def scatter_about(own_key, extent, width, limit, split=(), held_as=jnp.bfloat16):
    array = jax.random.normal(own_key, extent, jnp.float32) * width
    if len(split) > 0:
        array = block_scale(own_key, extent, split, -0.22, 0.18) * array
    return jnp.clip(array, min=-limit, max=limit).astype(held_as)


def setup_inputs(seed: int = 0, part: int = 0) -> dict:
    key_list = jax.random.split(jax.random.key(seed), 13)
    part_keys = jax.random.split(jax.random.fold_in(key_list[12], part), 13)
    vectors = scatter_about(part_keys[0], (NC, NV, LEAF), 1.0, 6.0, ((0, 4), (1, 4)))
    near_tiles = scatter_about(part_keys[1], (NB, LEAF, LEAF), (4 * LEAF) ** -0.5, 0.1875, ((0, 4),))
    self_tiles = scatter_about(part_keys[2], (NC, LEAF, LEAF), (4 * LEAF) ** -0.5, 0.1875, ((0, 4),))
    source_home_keys = jax.random.split(jax.random.fold_in(part_keys[3], 1), NB // BLK)
    source_home_turns = jax.random.permutation(jax.random.fold_in(part_keys[3], 3), NB // BLK)
    source_home = jax.vmap(lambda own, number: routed_block(jax.random.fold_in(part_keys[3], 2), own, number, BLK, N_LOOP, 1, SLOT, 1))(source_home_keys, source_home_turns).reshape((NB, 1))
    target_home_keys = jax.random.split(jax.random.fold_in(part_keys[4], 1), NB // BLK)
    target_home_turns = jax.random.permutation(jax.random.fold_in(part_keys[4], 3), NB // BLK)
    target_home = jax.vmap(lambda own, number: routed_block(jax.random.fold_in(part_keys[4], 2), own, number, BLK, N_LOOP, 1, SLOT, 1))(target_home_keys, target_home_turns).reshape((NB, 1))
    block_local = with_ends(jax.random.randint(part_keys[5], (NB, 2), 0, CL), jax.random.fold_in(part_keys[5], 1), 0, CL - 1).astype(jnp.int32)
    column_basis = scatter_about(part_keys[6], (NC, RANK, LEAF), LEAF ** -0.5, 0.375, ((0, 4),))
    row_basis = scatter_about(part_keys[7], (NC, RANK, LEAF), (4 * RANK) ** -0.5, 0.375, ((0, 4),))
    column_transfer = scatter_about(part_keys[8], (NC, RANK, RANK), (2 * RANK) ** -0.5, 0.5, ((0, 4),))
    row_transfer = scatter_about(part_keys[9], (NC, RANK, RANK), RANK ** -0.5, 0.75, ((0, 4),))
    coupling = scatter_about(part_keys[10], (NP, RANK, FAR * RANK), (FAR * RANK) ** -0.5, 0.25, ((0, 4),))
    far_source = with_ends(jax.random.randint(part_keys[11], (NP, FAR), 0, NP), jax.random.fold_in(part_keys[11], 1), 0, NP - 1).astype(jnp.int32)
    return {"vectors": vectors, "near_tiles": near_tiles, "self_tiles": self_tiles, "source_home": source_home, "target_home": target_home, "block_local": block_local, "column_basis": column_basis, "row_basis": row_basis, "column_transfer": column_transfer, "row_transfer": row_transfer, "coupling": coupling, "far_source": far_source}


PRECISE = lax.Precision.HIGHEST


def apply_once(current, near_tiles, self_tiles, source_index, target_index, column_basis, row_basis, column_transfer, row_transfer, coupling, far_source):
    wide = current.astype(jnp.float32)
    self_part = jnp.einsum("cvj,cij->cvi", wide, self_tiles.astype(jnp.float32), precision=PRECISE)
    panels = jnp.take(wide, source_index, axis=0)
    partials = jnp.einsum("bvj,bij->bvi", panels, near_tiles.astype(jnp.float32), precision=PRECISE)
    near_part = jax.ops.segment_sum(partials, target_index, num_segments=NC)
    leaf_coeffs = jnp.einsum("cvj,crj->cvr", wide, column_basis.astype(jnp.float32), precision=PRECISE)
    lifted = jnp.einsum("cvr,crs->cvs", leaf_coeffs, column_transfer.astype(jnp.float32), precision=PRECISE)
    parent_coeffs = jnp.sum(lifted.reshape(NP, 2, NV, RANK), axis=1).astype(jnp.bfloat16)
    gathered = jnp.take(parent_coeffs, far_source.reshape(-1), axis=0).reshape(NP, FAR, NV, RANK)
    parent_out = jnp.einsum("pfvj,pifj->pvi", gathered.astype(jnp.float32), coupling.reshape(NP, RANK, FAR, RANK).astype(jnp.float32), precision=PRECISE)
    leaf_out = jnp.einsum("cvr,crs->cvs", jnp.repeat(parent_out, 2, axis=0), row_transfer.astype(jnp.float32), precision=PRECISE).astype(jnp.bfloat16)
    far_part = jnp.einsum("cvr,cri->cvi", leaf_out.astype(jnp.float32), row_basis.astype(jnp.float32), precision=PRECISE)
    return (self_part + near_part + far_part).astype(jnp.bfloat16)


def reference(vectors, near_tiles, self_tiles, source_home, target_home, block_local, column_basis, row_basis, column_transfer, row_transfer, coupling, far_source):
    source_index = (source_home[:, 0] * CL + block_local[:, 0]).astype(jnp.int32)
    target_index = (target_home[:, 0] * CL + block_local[:, 1]).astype(jnp.int32)
    current = vectors
    for step in range(ITERS):
        current = apply_once(current, near_tiles, self_tiles, source_index, target_index, column_basis, row_basis, column_transfer, row_transfer, coupling, far_source)
    return current
```

```python
import functools

import jax
import jax.numpy as jnp
from jax import lax
from jax.experimental import pallas as pl
from jax.experimental.pallas import tpu as pltpu
from jax.sharding import PartitionSpec as P

ITERS = 2
F32, BF16 = jnp.float32, jnp.bfloat16
ROWS_BY_ROWS = (((1,), (1,)), ((), ()))
ROWS_BY_COLUMNS = (((1,), (0,)), ((), ()))
VMEM_LIMIT = 8 * 1024 * 1024


def dot(a, b, dims):
    return lax.dot_general(a, b, dims, preferred_element_type=F32)


def dot_wide(a, b, dims):
    rows = a.shape[0]
    upper = a.astype(BF16).astype(F32)
    halves = jnp.concatenate([upper, a - upper], axis=0).astype(BF16)
    both = dot(halves, b, dims)
    return both[:rows] + both[rows:]


def table_kernel(values, table, sem):
    copy = pltpu.make_async_copy(values, table, sem)
    copy.start()
    copy.wait()


def coeffs_kernel(current, column_basis, column_transfer, coeffs):
    for p in range(coeffs.shape[0]):
        total = None
        for c in (2 * p, 2 * p + 1):
            leaf = dot(current[c], column_basis[c], ROWS_BY_ROWS)
            lifted = dot_wide(leaf, column_transfer[c], ROWS_BY_COLUMNS)
            total = lifted if total is None else total + lifted
        coeffs[p] = jnp.concatenate([total, total], axis=-1).astype(BF16)


def self_kernel(current, self_tiles, self_part):
    for c in range(self_part.shape[0]):
        self_part[c] = dot(current[c], self_tiles[c], ROWS_BY_ROWS)


def near_kernel(panel_count, table, tiles, *refs):
    panels, (send, keep, gathered, products, sums) = refs[:panel_count], refs[panel_count:]
    clusters = panels[0].shape[0]
    blocks = tiles.shape[0]
    for k in range(panel_count):
        gathered[k * clusters : (k + 1) * clusters] = panels[k][...]
    sums[...] = jnp.zeros_like(sums)
    for b in range(blocks):
        products[b] = dot(gathered[table[b]], tiles[b], ROWS_BY_ROWS)
    for b in range(blocks):
        sums[table[blocks + b]] += products[b]
    half = send.shape[0]
    send[...] = sums[:half].astype(BF16)
    keep[...] = sums[half:]


def far_kernel(piece_count, first_entry, table, row_transfer, row_basis, coupling, *refs):
    pieces, (far_part, gathered) = refs[:piece_count], refs[piece_count:]
    parents, vectors, lanes = pieces[0].shape
    far_count = coupling.shape[2] // (lanes // 2)
    for k in range(piece_count):
        gathered[k * parents : (k + 1) * parents] = pieces[k][...]
    lower = lax.broadcasted_iota(jnp.int32, (vectors, lanes), 1) < lanes // 2
    for p in range(parents):
        pairs = []
        for f in range(0, far_count, 2):
            entry = first_entry + p * far_count + f
            first, second = gathered[table[entry]], gathered[table[entry + 1]]
            pairs.append(jnp.where(lower, first.astype(F32), second.astype(F32)).astype(BF16))
        inputs = jnp.concatenate(pairs, axis=-1)
        parent_out = dot(inputs, coupling[p], ROWS_BY_ROWS)
        for c in (2 * p, 2 * p + 1):
            leaf_out = dot_wide(parent_out, row_transfer[c], ROWS_BY_COLUMNS).astype(BF16)
            far_part[c] = dot(leaf_out, row_basis[c], ROWS_BY_COLUMNS)


def in_vmem(*arrays):
    return [pltpu.with_memory_space_constraint(a, pltpu.VMEM) for a in arrays]


VMEM_SPEC = pl.BlockSpec(memory_space=pltpu.VMEM)
SMEM_SPEC = pl.BlockSpec(memory_space=pltpu.SMEM)


def call(kernel, name, out_shape, in_specs, scratch_shapes=(), us=1.0):
    return pl.pallas_call(
        kernel,
        name=name,
        out_shape=out_shape,
        in_specs=in_specs,
        out_specs=jax.tree.map(lambda _: VMEM_SPEC, out_shape),
        scratch_shapes=scratch_shapes,
        compiler_params=pltpu.CompilerParams(vmem_limit_bytes=VMEM_LIMIT),
        cost_estimate=pl.CostEstimate(
            flops=int(us * 1.0e9), bytes_accessed=0, transcendentals=0
        ),
    )


def on_device(
    vectors,
    near_tiles,
    self_tiles,
    source_home,
    target_home,
    block_local,
    column_basis,
    row_basis,
    column_transfer,
    row_transfer,
    coupling,
    far_source,
):
    clusters, vector_count, leaf_size = vectors.shape
    blocks = near_tiles.shape[0]
    rank = column_basis.shape[1]
    parents, far_count = far_source.shape
    count = lax.axis_size("loop")
    columns = count // 2
    sibling = [(i, i ^ 1) for i in range(count)]

    def to_sibling(x):
        return lax.ppermute(x, "loop", sibling)

    def to_column(x, shift):
        return lax.ppermute(x, "loop", [(i, (i + 2 * shift) % count) for i in range(count)])

    def gather(x):
        near = [x] + [to_column(x, s) for s in range(1, columns)]
        return [piece for y in near for piece in (y, to_sibling(y))]

    panel = (clusters, vector_count, leaf_size)
    coeffs_shape = (parents, vector_count, 2 * rank)
    sums_shape = (columns * clusters, vector_count, leaf_size)

    me = lax.axis_index("loop")
    my_column, my_core = me // 2, me % 2

    def piece(home, local, size):
        shift = (my_column - home // 2) % columns
        return (2 * shift + (home % 2 != my_core)) * size + local

    source, target = source_home[:, 0], target_home[:, 0]
    target_place = ((target // 2 - my_column) % columns) * clusters + block_local[:, 1]
    values = jnp.concatenate(
        [
            piece(source, block_local[:, 0], clusters),
            target_place + jnp.where(target % 2 == my_core, columns * clusters, 0),
            piece(far_source // parents, far_source % parents, parents).reshape(-1),
        ]
    )
    table = pl.pallas_call(
        table_kernel,
        name="table",
        out_shape=pltpu.SMEM(values.shape, jnp.int32),
        in_specs=[pl.BlockSpec(memory_space=pl.ANY)],
        out_specs=SMEM_SPEC,
        scratch_shapes=[pltpu.SemaphoreType.DMA],
    )(values)

    def with_table(x):
        return pltpu.with_memory_space_constraint(x, pltpu.SMEM)

    coeffs_call = call(
        coeffs_kernel, "coeffs", jax.ShapeDtypeStruct(coeffs_shape, BF16), [VMEM_SPEC] * 3
    )
    self_call = call(self_kernel, "self", jax.ShapeDtypeStruct(panel, F32), [VMEM_SPEC] * 2)
    near_call = call(
        functools.partial(near_kernel, count),
        "near",
        (jax.ShapeDtypeStruct(sums_shape, BF16), jax.ShapeDtypeStruct(sums_shape, F32)),
        [SMEM_SPEC] + [VMEM_SPEC] * (1 + count),
        [
            pltpu.VMEM((count * clusters, vector_count, leaf_size), BF16),
            pltpu.VMEM((blocks, vector_count, leaf_size), F32),
            pltpu.VMEM((count * clusters, vector_count, leaf_size), F32),
        ],
    )
    far_call = call(
        functools.partial(far_kernel, count, 2 * blocks),
        "far",
        jax.ShapeDtypeStruct(panel, F32),
        [SMEM_SPEC] + [VMEM_SPEC] * (3 + count),
        [pltpu.VMEM((count * parents, vector_count, 2 * rank), BF16)],
    )

    current = vectors
    for step in range(ITERS):
        panels = gather(current)
        coeffs = coeffs_call(*in_vmem(current, column_basis, column_transfer))
        self_part = self_call(*in_vmem(current, self_tiles))
        pieces = gather(coeffs)
        send, keep = near_call(with_table(table), *in_vmem(near_tiles, *panels))
        far_part = far_call(
            with_table(table), *in_vmem(row_transfer, row_basis, coupling, *pieces)
        )
        arrived = to_sibling(send).reshape(columns, *panel)
        keep = keep.reshape(columns, *panel)
        near = keep[0] + arrived[0].astype(F32)
        for s in range(1, columns):
            partial = (keep[s] + arrived[s].astype(F32)).astype(BF16)
            near = near + to_column(partial, s).astype(F32)
        current = (self_part + far_part + near).astype(BF16)
    return current


def solution(mesh):
    in_specs = (
        P(("groups", "loop"), "cuts", None),
        P(("groups", "loop"), None, None),
        P(("groups", "loop"), None, None),
        P(("groups", "loop"), None),
        P(("groups", "loop"), None),
        P(("groups", "loop"), None),
        P(("groups", "loop"), None, None),
        P(("groups", "loop"), None, None),
        P(("groups", "loop"), None, None),
        P(("groups", "loop"), None, None),
        P(("groups", "loop"), None, None),
        P(("groups", "loop"), None),
    )
    out_specs = P(("groups", "loop"), "cuts", None)
    return jax.shard_map(
        on_device, mesh=mesh, in_specs=in_specs, out_specs=out_specs, check_vma=False
    )
```

```python
import functools

import jax
import jax.numpy as jnp
from jax import lax
from jax.experimental import pallas as pl
from jax.experimental.pallas import tpu as pltpu
from jax.sharding import PartitionSpec as P

ITERS = 2
F32, BF16 = jnp.float32, jnp.bfloat16
ROWS_BY_ROWS = (((1,), (1,)), ((), ()))
ROWS_BY_COLUMNS = (((1,), (0,)), ((), ()))
VMEM_LIMIT = 12 * 1024 * 1024
CHUNKS = 4


def dot(a, b, dims):
    return lax.dot_general(a, b, dims, preferred_element_type=F32)


def dot_wide(a, b, dims):
    rows = a.shape[0]
    upper = a.astype(BF16).astype(F32)
    halves = jnp.concatenate([upper, a - upper], axis=0).astype(BF16)
    both = dot(halves, b, dims)
    return both[:rows] + both[rows:]


def lanes_below(vectors, lanes):
    return lax.broadcasted_iota(jnp.int32, (vectors, lanes), 1) < lanes // 2


def parent_coeffs(current, column_basis, column_transfer, coeffs):
    parents, vectors, lanes = coeffs.shape
    rank, leaf_size = column_basis.shape[1:]
    lower = lanes_below(vectors, lanes)
    leaves = []
    for p in range(parents):
        both = dot(
            current[2 * p : 2 * p + 2].reshape(2 * vectors, leaf_size),
            column_basis[2 * p : 2 * p + 2].reshape(2 * rank, leaf_size),
            ROWS_BY_ROWS,
        )
        leaves.append(jnp.where(lower, both[:vectors], both[vectors:]))
    for p in range(parents):
        transfer = column_transfer[2 * p : 2 * p + 2].reshape(2 * rank, rank)
        total = dot_wide(leaves[p], transfer, ROWS_BY_COLUMNS)
        coeffs[p] = jnp.concatenate([total, total], axis=-1).astype(BF16)


def self_product(current, self_tiles, self_part):
    for c in range(self_part.shape[0]):
        self_part[c] = dot(current[c], self_tiles[c], ROWS_BY_ROWS)


def fill_table(me, columns, clusters, parents, raw, table):
    source_home, target_home, block_local, far_source = raw
    my_column = me // 2
    blocks = source_home.shape[1]

    def around(shift):
        return jnp.where(shift < 0, shift + columns, shift)

    for b in range(blocks):
        home = source_home[0, b]
        shift = around(my_column - home // 2)
        table[b] = (2 * shift + ((home ^ me) & 1)) * clusters + block_local[0, b]
        home = target_home[0, b]
        shift = around(home // 2 - my_column)
        same = 1 - ((home ^ me) & 1)
        table[blocks + b] = (same * columns + shift) * clusters + block_local[1, b]
    far_count = far_source.shape[1]
    for p in range(parents):
        for f in range(far_count):
            home = lax.div(far_source[p, f], parents)
            local = lax.rem(far_source[p, f], parents)
            shift = around(my_column - home // 2)
            entry = 2 * blocks + p * far_count + f
            table[entry] = (2 * shift + ((home ^ me) & 1)) * parents + local


def load_all(sems, *pairs):
    copies = [pltpu.make_async_copy(x, y, sems.at[i]) for i, (x, y) in enumerate(pairs)]
    for copy in copies:
        copy.start()
    return copies


def turn(staged, held, copies):
    each = staged.shape[0] // len(copies)
    for k, copy in enumerate(copies):
        copy.wait()
        for b in range(k * each, (k + 1) * each):
            held[b] = staged[b].T


def tile_pairs(tiles, first, staged):
    each = staged.shape[0] // CHUNKS
    return [
        (tiles.at[pl.ds(first + k * each, each)], staged.at[pl.ds(k * each, each)])
        for k in range(CHUNKS)
    ]


def first_kernel(
    vectors,
    column_basis,
    column_transfer,
    tiles,
    coeffs,
    current,
    basis_held,
    transfer_held,
    held,
    staged,
    sems,
):
    copies = load_all(
        sems,
        (vectors, current),
        (column_basis, basis_held),
        (column_transfer, transfer_held),
        *tile_pairs(tiles, 0, staged),
    )
    for copy in copies[:3]:
        copy.wait()
    parent_coeffs(current, basis_held, transfer_held, coeffs)
    turn(staged, held, copies[3:])


def load_kernel(
    columns,
    clusters,
    source_home,
    target_home,
    block_local,
    far_source,
    tiles,
    held,
    table,
    staged,
    source_smem,
    target_smem,
    local_smem,
    far_smem,
    sems,
):
    raw = (source_smem, target_smem, local_smem, far_smem)
    given = (source_home, target_home, block_local, far_source)
    copies = load_all(sems, *zip(given, raw), *tile_pairs(tiles, held.shape[0], staged))
    for copy in copies[:4]:
        copy.wait()
    fill_table(lax.axis_index("loop"), columns, clusters, far_source.shape[0], raw, table)
    turn(staged, held, copies[4:])


def next_kernel(current, column_basis, column_transfer, coeffs):
    parent_coeffs(current, column_basis, column_transfer, coeffs)


def self_kernel(current, self_tiles, self_part):
    self_product(current, self_tiles, self_part)


def tie_kernel(*refs):
    pass


def near_kernel(panel_count, part_count, table, *refs):
    parts, refs = refs[:part_count], refs[part_count:]
    panels, (send, keep, gathered, products, sums) = refs[:panel_count], refs[-5:]
    row = 0
    for panel in panels:
        gathered[row : row + panel.shape[0]] = panel[...]
        row += panel.shape[0]
    sums[...] = jnp.zeros_like(sums)
    b = 0
    for tiles in parts:
        for k in range(tiles.shape[0]):
            products[b] = dot(gathered[table[b]], tiles[k], ROWS_BY_COLUMNS)
            b += 1
    for k in range(b):
        sums[table[b + k]] += products[k]
    half = send.shape[0]
    send[...] = sums[:half].astype(BF16)
    keep[...] = sums[half:]


def join_kernel(keep, arrived, self_part, far_part, message, sums):
    half = self_part.shape[0]
    other = keep[half:] + arrived[half:].astype(F32)
    own = keep[:half] + arrived[:half].astype(F32) + self_part[...] + far_part[...]
    sums[:half] = own
    sums[half:] = other
    message[:half] = other.astype(BF16)
    message[half:] = own.astype(BF16)


def settle_kernel(sums, message, pair):
    pair[...] = (sums[...] + message[...].astype(F32)).astype(BF16)


def far_products(
    pieces, first_entry, table, row_transfer, row_basis, coupling, gathered, store
):
    row = 0
    for piece in pieces:
        gathered[row : row + piece.shape[0]] = piece[...]
        row += piece.shape[0]
    vectors, lanes = gathered.shape[1:]
    rank, leaf_size = row_basis.shape[1:]
    parents = coupling.shape[0]
    far_count = coupling.shape[2] // rank
    lower = lanes_below(vectors, lanes)
    parent_outs = []
    for p in range(parents):
        pairs = []
        for f in range(0, far_count, 2):
            entry = first_entry + p * far_count + f
            first, second = gathered[table[entry]], gathered[table[entry + 1]]
            pairs.append(jnp.where(lower, first.astype(F32), second.astype(F32)).astype(BF16))
        parent_outs.append(dot(jnp.concatenate(pairs, axis=-1), coupling[p], ROWS_BY_ROWS))
    leaf_outs = []
    for p in range(parents):
        transfer = jnp.concatenate([row_transfer[2 * p], row_transfer[2 * p + 1]], axis=-1)
        leaf_outs.append(dot_wide(parent_outs[p], transfer, ROWS_BY_COLUMNS))
    for p in range(parents):
        zero = jnp.zeros_like(leaf_outs[p])
        stacked = jnp.concatenate(
            [jnp.where(lower, leaf_outs[p], zero), jnp.where(lower, zero, leaf_outs[p])], axis=0
        ).astype(BF16)
        basis = row_basis[2 * p : 2 * p + 2].reshape(2 * rank, leaf_size)
        both = dot(stacked, basis, ROWS_BY_COLUMNS)
        store(2 * p, both.reshape(2, vectors, leaf_size))


def far_kernel(piece_count, first_entry, table, row_transfer, row_basis, coupling, *refs):
    pieces, (far_part, gathered) = refs[:piece_count], refs[piece_count:]

    def store(c, both):
        far_part[c : c + 2] = both

    far_products(
        pieces, first_entry, table, row_transfer, row_basis, coupling, gathered, store
    )


def widen_kernel(keep, arrived, coeffs, beside, message):
    half = keep.shape[0] // 2
    message[:half] = (keep[half:] + arrived[half:].astype(F32)).astype(BF16)
    parents, _, lanes = coeffs.shape
    each = message.shape[2] // (lanes // 2)
    row = half
    for one in (coeffs, beside):
        for p in range(0, parents, each):
            parts = [one[p + k][:, : lanes // 2] for k in range(each)]
            message[row] = jnp.concatenate(parts, axis=-1)
            row += 1


def last_kernel(
    first_entry,
    table,
    row_transfer,
    row_basis,
    coupling,
    coeffs,
    beside,
    self_part,
    keep,
    arrived,
    message,
    product,
    gathered,
    unpacked,
):
    clusters = self_part.shape[0]
    _, vectors, lanes = coeffs.shape
    width = lanes // 2
    each = message.shape[2] // width
    for row in range(clusters, message.shape[0]):
        for k in range(each):
            part = message[row][:, k * width : (k + 1) * width]
            unpacked[(row - clusters) * each + k] = jnp.concatenate([part, part], axis=-1)

    def store(c, both):
        near = keep[c : c + 2] + arrived[c : c + 2].astype(F32) + message[c : c + 2].astype(F32)
        product[c : c + 2] = (self_part[c : c + 2] + both + near).astype(BF16)

    far_products(
        (coeffs, beside, unpacked),
        first_entry,
        table,
        row_transfer,
        row_basis,
        coupling,
        gathered,
        store,
    )


def in_vmem(*arrays):
    return [pltpu.with_memory_space_constraint(a, pltpu.VMEM) for a in arrays]


def in_hbm(*arrays):
    return [pltpu.with_memory_space_constraint(a, pltpu.HBM) for a in arrays]


VMEM_SPEC = pl.BlockSpec(memory_space=pltpu.VMEM)
HBM_SPEC = pl.BlockSpec(memory_space=pltpu.HBM)
ANY_SPEC = pl.BlockSpec(memory_space=pl.ANY)
SMEM_SPEC = pl.BlockSpec(memory_space=pltpu.SMEM)


def call(kernel, name, out_shape, in_specs, scratch_shapes=(), out_specs=None, us=1.0):
    return pl.pallas_call(
        kernel,
        name=name,
        out_shape=out_shape,
        in_specs=in_specs,
        out_specs=jax.tree.map(lambda _: VMEM_SPEC, out_shape) if out_specs is None else out_specs,
        scratch_shapes=scratch_shapes,
        compiler_params=pltpu.CompilerParams(vmem_limit_bytes=VMEM_LIMIT),
        cost_estimate=pl.CostEstimate(
            flops=int(us * 1.0e9), bytes_accessed=0, transcendentals=0
        ),
    )


def on_device(
    vectors,
    near_tiles,
    self_tiles,
    source_home,
    target_home,
    block_local,
    column_basis,
    row_basis,
    column_transfer,
    row_transfer,
    coupling,
    far_source,
):
    clusters, vector_count, leaf_size = vectors.shape
    blocks = near_tiles.shape[0]
    rank = column_basis.shape[1]
    parents, far_count = far_source.shape
    count = lax.axis_size("loop")
    columns = count // 2
    sibling = [(i, i ^ 1) for i in range(count)]

    def to_sibling(x):
        return lax.ppermute(x, "loop", sibling)

    def to_column(x, shift):
        return lax.ppermute(x, "loop", [(i, (i + 2 * shift) % count) for i in range(count)])

    panel = (clusters, vector_count, leaf_size)
    coeffs_shape = (parents, vector_count, 2 * rank)
    sums_shape = (columns * clusters, vector_count, leaf_size)

    def with_table(x):
        return pltpu.with_memory_space_constraint(x, pltpu.SMEM)

    held = (vectors, column_basis, column_transfer)
    entries = 2 * blocks + parents * far_count
    coeffs_out = jax.ShapeDtypeStruct(coeffs_shape, BF16)
    panel_out = jax.ShapeDtypeStruct(panel, F32)
    half_tiles = pltpu.VMEM((blocks // 2, leaf_size, leaf_size), BF16)
    first_call = call(
        first_kernel,
        "first",
        (coeffs_out, *(pltpu.VMEM(x.shape, x.dtype) for x in held), half_tiles),
        [HBM_SPEC] * 4,
        [half_tiles, pltpu.SemaphoreType.DMA((3 + CHUNKS,))],
        us=3.0,
    )
    raw = (source_home.T, target_home.T, block_local.T, far_source)
    load_call = call(
        functools.partial(load_kernel, columns, clusters),
        "load",
        (half_tiles, pltpu.SMEM((entries,), jnp.int32)),
        [HBM_SPEC] * 5,
        [half_tiles]
        + [pltpu.SMEM(x.shape, x.dtype) for x in raw]
        + [pltpu.SemaphoreType.DMA((4 + CHUNKS,))],
        out_specs=(VMEM_SPEC, SMEM_SPEC),
        us=2.0,
    )
    next_call = call(next_kernel, "next", coeffs_out, [VMEM_SPEC] * 3, us=0.5)
    self_call = call(self_kernel, "self", panel_out, [VMEM_SPEC] * 2, us=0.5)
    message_out = jax.ShapeDtypeStruct((2 * clusters, vector_count, leaf_size), BF16)
    join_call = call(
        join_kernel,
        "join",
        (message_out, jax.ShapeDtypeStruct(message_out.shape, F32)),
        [VMEM_SPEC] * 4,
        us=0.1,
    )
    settle_call = call(settle_kernel, "settle", message_out, [VMEM_SPEC] * 2, us=0.1)
    sums_out = (jax.ShapeDtypeStruct(sums_shape, BF16), jax.ShapeDtypeStruct(sums_shape, F32))
    near_scratch = [
        pltpu.VMEM((count * clusters, vector_count, leaf_size), BF16),
        pltpu.VMEM((blocks, vector_count, leaf_size), F32),
        pltpu.VMEM((count * clusters, vector_count, leaf_size), F32),
    ]

    def near_call(panels, others):
        return call(
            functools.partial(near_kernel, len(panels), len(tiles)),
            "near",
            sums_out,
            [SMEM_SPEC]
            + [VMEM_SPEC] * (len(tiles) + len(panels))
            + [ANY_SPEC] * len(others),
            near_scratch,
            us=1.0,
        )(with_table(table), *in_vmem(*tiles, *panels), *others)

    gathered_coeffs = pltpu.VMEM((count * parents, vector_count, 2 * rank), BF16)
    far_call = call(
        functools.partial(far_kernel, count, 2 * blocks),
        "far",
        panel_out,
        [SMEM_SPEC] + [VMEM_SPEC] * (3 + count),
        [gathered_coeffs],
        us=0.5,
    )
    packed = 2 * parents * rank // leaf_size
    wide_out = jax.ShapeDtypeStruct((clusters + packed, vector_count, leaf_size), BF16)
    widen_call = call(widen_kernel, "widen", wide_out, [VMEM_SPEC] * 4, us=0.1)
    last_call = call(
        functools.partial(last_kernel, 2 * blocks),
        "last",
        jax.ShapeDtypeStruct(panel, BF16),
        [SMEM_SPEC] + [VMEM_SPEC] * 9,
        [gathered_coeffs, pltpu.VMEM((2 * parents, vector_count, 2 * rank), BF16)],
        us=0.6,
    )

    def tie(x, *others):
        return pl.pallas_call(
            tie_kernel,
            name="tie",
            out_shape=pltpu.VMEM(x.shape, x.dtype),
            in_specs=[VMEM_SPEC] + [pl.BlockSpec(memory_space=pl.ANY)] * len(others),
            out_specs=VMEM_SPEC,
            input_output_aliases={0: 0},
            compiler_params=pltpu.CompilerParams(vmem_limit_bytes=VMEM_LIMIT),
        )(*in_vmem(x), *others)

    def far_of(near_coeffs):
        pieces = [piece for x in near_coeffs for piece in (x, to_sibling(x))]
        return far_call(
            with_table(table), *in_vmem(row_transfer, row_basis, coupling, *pieces)
        )

    def across(x):
        return [to_column(x, shift) for shift in range(1, columns)]

    def gathered(current, from_columns, beside, coeffs):
        panels = [current, beside]
        for x in from_columns:
            panels += [x, to_sibling(tie(x, coeffs))]
        return panels

    def finished(keep, arrived, self_part, far_part):
        near = keep[:clusters] + arrived[:clusters].astype(F32)
        for s in range(1, columns):
            rows = slice(s * clusters, (s + 1) * clusters)
            partial = (keep[rows] + arrived[rows].astype(F32)).astype(BF16)
            near = near + to_column(partial, s).astype(F32)
        return (self_part + far_part + near).astype(BF16)

    from_columns = across(vectors)
    beside = to_sibling(vectors)
    coeffs, current, basis_held, transfer_held, first_half = first_call(
        *in_hbm(*held, near_tiles)
    )
    second_half, table = load_call(*in_hbm(*raw, near_tiles))
    tiles = (first_half, second_half)
    near_coeffs = [coeffs] + across(coeffs)
    panels = gathered(current, from_columns, beside, coeffs)
    send, keep = near_call(panels, near_coeffs)
    arrived = to_sibling(send)
    self_part = self_call(*in_vmem(current, self_tiles))
    far_part = far_of(near_coeffs)

    if columns == 2 and ITERS == 2:
        message, sums = join_call(*in_vmem(keep, arrived, self_part, far_part))
        pair = settle_call(*in_vmem(sums, to_column(message, 1)))
        beside = to_sibling(pair)
        current = pair[:clusters]
        coeffs = next_call(*in_vmem(current, basis_held, transfer_held))
        panels = [pair[:clusters], beside[:clusters], pair[clusters:], beside[clusters:]]
        send, keep = near_call(panels, [coeffs])
        arrived = to_sibling(send)
        coeffs_beside = to_sibling(coeffs)
        self_part = self_call(*in_vmem(current, self_tiles))
        message = widen_call(*in_vmem(keep, arrived, coeffs, coeffs_beside))
        return last_call(
            with_table(table),
            *in_vmem(
                row_transfer,
                row_basis,
                coupling,
                coeffs,
                coeffs_beside,
                self_part,
                keep,
                arrived,
                to_column(message, 1),
            ),
        )
    for step in range(1, ITERS):
        current = finished(keep, arrived, self_part, far_part)
        from_columns = across(current)
        beside = to_sibling(current)
        coeffs = next_call(*in_vmem(current, basis_held, transfer_held))
        near_coeffs = [coeffs] + across(coeffs)
        panels = gathered(current, from_columns, beside, coeffs)
        send, keep = near_call(panels, near_coeffs)
        arrived = to_sibling(send)
        self_part = self_call(*in_vmem(current, self_tiles))
        far_part = far_of(near_coeffs)
    return finished(keep, arrived, self_part, far_part)


def solution(mesh):
    in_specs = (
        P(("groups", "loop"), "cuts", None),
        P(("groups", "loop"), None, None),
        P(("groups", "loop"), None, None),
        P(("groups", "loop"), None),
        P(("groups", "loop"), None),
        P(("groups", "loop"), None),
        P(("groups", "loop"), None, None),
        P(("groups", "loop"), None, None),
        P(("groups", "loop"), None, None),
        P(("groups", "loop"), None, None),
        P(("groups", "loop"), None, None),
        P(("groups", "loop"), None),
    )
    out_specs = P(("groups", "loop"), "cuts", None)
    return jax.shard_map(
        on_device, mesh=mesh, in_specs=in_specs, out_specs=out_specs, check_vma=False
    )
```

```python
import functools

import jax
import jax.numpy as jnp
from jax import lax
from jax.experimental import pallas as pl
from jax.experimental.pallas import tpu as pltpu
from jax.sharding import PartitionSpec as P

ITERS = 2
F32, BF16 = jnp.float32, jnp.bfloat16
ROWS_BY_ROWS = (((1,), (1,)), ((), ()))
ROWS_BY_COLUMNS = (((1,), (0,)), ((), ()))
VMEM_LIMIT = 8 * 1024 * 1024
FAR_ROW = 8


def dot(a, b, dims):
    return lax.dot_general(a, b, dims, preferred_element_type=F32)


def dot_wide(a, b, dims):
    rows = a.shape[0]
    upper = a.astype(BF16).astype(F32)
    halves = jnp.concatenate([upper, a - upper], axis=0).astype(BF16)
    both = dot(halves, b, dims)
    return both[:rows] + both[rows:]


def lanes_below(vectors, lanes):
    return lax.broadcasted_iota(jnp.int32, (vectors, lanes), 1) < lanes // 2


def load_all(sems, *pairs):
    copies = [pltpu.make_async_copy(x, y, sems.at[i]) for i, (x, y) in enumerate(pairs)]
    for copy in copies:
        copy.start()
    return copies


def parent_coeffs(current, column_basis, column_transfer, packed, first):
    clusters, rank, leaf_size = column_basis.shape
    vectors = current.shape[1]
    parents = clusters // 2
    lower = lanes_below(vectors, 2 * rank)
    leaves = []
    for p in range(parents):
        both = dot(
            current[2 * p : 2 * p + 2].reshape(2 * vectors, leaf_size),
            column_basis[2 * p : 2 * p + 2].reshape(2 * rank, leaf_size),
            ROWS_BY_ROWS,
        )
        leaves.append(jnp.where(lower, both[:vectors], both[vectors:]))
    totals = []
    for p in range(parents):
        transfer = column_transfer[2 * p : 2 * p + 2].reshape(2 * rank, rank)
        totals.append(dot_wide(leaves[p], transfer, ROWS_BY_COLUMNS))
    each = leaf_size // rank
    for p in range(0, parents, each):
        row = jnp.concatenate(totals[p : p + each], axis=-1)
        packed[first + p // each] = row.astype(BF16)


def unpack(packed, first, rows, rank, gathered, slot):
    for r in range(rows):
        row = packed[first + r].astype(F32)
        for k in range(row.shape[1] // (2 * rank)):
            pair = row[:, 2 * rank * k : 2 * rank * (k + 1)]
            lower = lanes_below(*pair.shape)
            turned = pltpu.roll(pair, rank, 1)
            gathered[slot] = jnp.where(lower, pair, turned).astype(BF16)
            gathered[slot + 1] = jnp.where(lower, turned, pair).astype(BF16)
            slot += 2
    return slot


def place_table(columns, clusters, source, target, local, far, values):
    me = lax.axis_index("loop")
    my_column = me // 2

    def around(shift):
        return jnp.where(shift < 0, shift + columns, shift)

    def other_core(home):
        return (home ^ me) & 1

    blocks = source.shape[1]
    home = source[...]
    shift = around(my_column - (home >> 1))
    values[0:1, :blocks] = (2 * shift + other_core(home)) * clusters + local[0:1]
    home = target[...]
    shift = around((home >> 1) - my_column)
    values[1:2, :blocks] = ((1 - other_core(home)) * columns + shift) * clusters + local[1:2]
    cluster = far[...]
    parents, far_count = cluster.shape
    home = jnp.zeros_like(cluster)
    for h in range(1, 2 * columns):
        home = home + jnp.where(cluster >= h * parents, 1, 0)
    shift = around(my_column - (home >> 1))
    place = (2 * shift + other_core(home)) * parents + cluster - home * parents
    values[FAR_ROW : FAR_ROW + parents, :far_count] = place


def first_kernel(
    columns,
    source_home,
    target_home,
    block_local,
    far_source,
    vectors,
    column_basis,
    column_transfer,
    packed,
    current,
    table,
    basis_held,
    transfer_held,
    source,
    target,
    local,
    far,
    values,
    sems,
):
    copies = load_all(
        sems,
        (source_home, source),
        (target_home, target),
        (block_local, local),
        (far_source, far),
        (vectors, current),
        (column_basis, basis_held),
        (column_transfer, transfer_held),
    )
    for copy in copies[:4]:
        copy.wait()
    place_table(columns, vectors.shape[0], source, target, local, far, values)
    placed = pltpu.make_async_copy(values, table, sems.at[7])
    placed.start()
    for copy in copies[4:]:
        copy.wait()
    parent_coeffs(current, basis_held, transfer_held, packed, 0)
    placed.wait()


def coeffs_kernel(current, column_basis, column_transfer, packed):
    parent_coeffs(current, column_basis, column_transfer, packed, 0)


def message_kernel(current, column_basis, column_transfer, message):
    clusters = current.shape[0]
    message[:clusters] = current[...]
    parent_coeffs(current, column_basis, column_transfer, message, clusters)


def self_kernel(current, self_tiles, *others):
    self_part = others[-1]
    for c in range(self_part.shape[0]):
        self_part[c] = dot(current[c], self_tiles[c], ROWS_BY_ROWS)


def turn_kernel(tiles, turned):
    for b in range(tiles.shape[0]):
        turned[b] = tiles[b].T


def near_kernel(panel_count, table, tiles, *refs):
    panels, refs = refs[:panel_count], refs[panel_count:]
    send, send_own, keep, keep_own, gathered, products, sums = refs[-7:]
    each = gathered.shape[0] // panel_count
    for k, panel in enumerate(panels):
        gathered[k * each : (k + 1) * each] = panel[:each]
    sums[...] = jnp.zeros_like(sums)
    blocks = tiles.shape[0]
    for b in range(blocks):
        products[b] = dot(gathered[table[0, b]], tiles[b], ROWS_BY_COLUMNS)
    for b in range(blocks):
        sums[table[1, b]] += products[b]
    own, half = keep_own.shape[0], sums.shape[0] // 2
    send_own[...] = sums[:own].astype(BF16)
    send[...] = sums[own:half].astype(BF16)
    keep_own[...] = sums[half : half + own]
    keep[...] = sums[half + own :]


def far_products(table, row_transfer, row_basis, coupling, gathered, store):
    vectors, lanes = gathered.shape[1:]
    rank, leaf_size = row_basis.shape[1:]
    parents = coupling.shape[0]
    far_count = coupling.shape[2] // rank
    lower = lanes_below(vectors, lanes)
    parent_outs = []
    for p in range(parents):
        pairs = []
        for f in range(0, far_count, 2):
            first = gathered[table[FAR_ROW + p, f]]
            second = gathered[table[FAR_ROW + p, f + 1]]
            pairs.append(jnp.where(lower, first.astype(F32), second.astype(F32)).astype(BF16))
        parent_outs.append(dot(jnp.concatenate(pairs, axis=-1), coupling[p], ROWS_BY_ROWS))
    leaf_outs = []
    for p in range(parents):
        transfer = jnp.concatenate([row_transfer[2 * p], row_transfer[2 * p + 1]], axis=-1)
        leaf_outs.append(dot_wide(parent_outs[p], transfer, ROWS_BY_COLUMNS))
    for p in range(parents):
        zero = jnp.zeros_like(leaf_outs[p])
        stacked = jnp.concatenate(
            [jnp.where(lower, leaf_outs[p], zero), jnp.where(lower, zero, leaf_outs[p])], axis=0
        ).astype(BF16)
        basis = row_basis[2 * p : 2 * p + 2].reshape(2 * rank, leaf_size)
        both = dot(stacked, basis, ROWS_BY_COLUMNS)
        store(2 * p, both.reshape(2, vectors, leaf_size))


def far_kernel(message_count, rows, table, row_transfer, row_basis, coupling, *refs):
    messages, (far_part, gathered) = refs[:message_count], refs[-2:]
    slot = 0
    for message in messages:
        slot = unpack(message, message.shape[0] - rows, rows, row_basis.shape[1], gathered, slot)

    def store(c, both):
        far_part[c : c + 2] = both

    far_products(table, row_transfer, row_basis, coupling, gathered, store)


def other_kernel(keep, arrived, message, sums):
    other = keep[...] + arrived[...].astype(F32)
    sums[...] = other
    message[...] = other.astype(BF16)


def own_kernel(keep, arrived, self_part, far_part, sent_before, message, sums):
    own = keep[...] + arrived[...].astype(F32) + self_part[...] + far_part[...]
    sums[...] = own
    message[...] = own.astype(BF16)


def settle_kernel(sums, message, *others):
    current = others[-1]
    current[...] = (sums[...] + message[...].astype(F32)).astype(BF16)


def cross_kernel(keep, arrived, self_part, column_coeffs, message):
    message[...] = (keep[...] + arrived[...].astype(F32)).astype(BF16)


def last_kernel(self_part, far_part, keep, arrived, message, product):
    near = keep[...] + arrived[...].astype(F32) + message[...].astype(F32)
    product[...] = (self_part[...] + far_part[...] + near).astype(BF16)


def tie_kernel(*refs):
    pass


def in_vmem(*arrays):
    return [pltpu.with_memory_space_constraint(a, pltpu.VMEM) for a in arrays]


def in_hbm(*arrays):
    return [pltpu.with_memory_space_constraint(a, pltpu.HBM) for a in arrays]


def in_smem(array):
    return pltpu.with_memory_space_constraint(array, pltpu.SMEM)


VMEM_SPEC = pl.BlockSpec(memory_space=pltpu.VMEM)
HBM_SPEC = pl.BlockSpec(memory_space=pltpu.HBM)
ANY_SPEC = pl.BlockSpec(memory_space=pl.ANY)
SMEM_SPEC = pl.BlockSpec(memory_space=pltpu.SMEM)


def call(kernel, name, out_shape, in_specs, scratch_shapes=(), out_specs=None, us=1.0):
    return pl.pallas_call(
        kernel,
        name=name,
        out_shape=out_shape,
        in_specs=in_specs,
        out_specs=jax.tree.map(lambda _: VMEM_SPEC, out_shape) if out_specs is None else out_specs,
        scratch_shapes=scratch_shapes,
        compiler_params=pltpu.CompilerParams(vmem_limit_bytes=VMEM_LIMIT),
        cost_estimate=pl.CostEstimate(
            flops=int(us * 1.0e9), bytes_accessed=0, transcendentals=0
        ),
    )


def tie(x, *others):
    return pl.pallas_call(
        tie_kernel,
        name="tie",
        out_shape=pltpu.VMEM(x.shape, x.dtype),
        in_specs=[VMEM_SPEC] + [ANY_SPEC] * len(others),
        out_specs=VMEM_SPEC,
        input_output_aliases={0: 0},
        compiler_params=pltpu.CompilerParams(vmem_limit_bytes=VMEM_LIMIT),
    )(*in_vmem(x), *others)


def on_device(
    vectors,
    near_tiles,
    self_tiles,
    source_home,
    target_home,
    block_local,
    column_basis,
    row_basis,
    column_transfer,
    row_transfer,
    coupling,
    far_source,
):
    clusters, vector_count, leaf_size = vectors.shape
    blocks = near_tiles.shape[0]
    rank = column_basis.shape[1]
    parents, far_count = far_source.shape
    count = lax.axis_size("loop")
    columns = count // 2
    sibling = [(i, i ^ 1) for i in range(count)]

    def to_sibling(x):
        return lax.ppermute(x, "loop", sibling)

    def to_column(x, shift):
        return lax.ppermute(x, "loop", [(i, (i + 2 * shift) % count) for i in range(count)])

    def across(x):
        return [to_column(x, shift) for shift in range(1, columns)]

    def panels(number, dtype):
        return jax.ShapeDtypeStruct((number, vector_count, leaf_size), dtype)

    def scratch(number, dtype, width=leaf_size):
        return pltpu.VMEM((number, vector_count, width), dtype)

    rows = parents * rank // leaf_size
    raw = (source_home.T, target_home.T, block_local.T, far_source)
    table_shape = (FAR_ROW + parents, 128)
    first_call = call(
        functools.partial(first_kernel, columns),
        "first",
        (
            panels(rows, BF16),
            pltpu.VMEM(vectors.shape, BF16),
            pltpu.SMEM(table_shape, jnp.int32),
        ),
        [HBM_SPEC] * 7,
        [pltpu.VMEM(x.shape, x.dtype) for x in (column_basis, column_transfer, *raw)]
        + [pltpu.VMEM(table_shape, jnp.int32), pltpu.SemaphoreType.DMA((8,))],
        out_specs=(VMEM_SPEC, VMEM_SPEC, SMEM_SPEC),
        us=10.0,
    )
    turn_call = call(
        turn_kernel, "turn", pltpu.VMEM(near_tiles.shape, BF16), [VMEM_SPEC], us=2.5
    )
    coeffs_call = call(coeffs_kernel, "coeffs", panels(rows, BF16), [VMEM_SPEC] * 3, us=0.5)
    def self_call(current, *others, us=0.6):
        specs = [VMEM_SPEC] * 2 + [ANY_SPEC] * len(others)
        return call(self_kernel, "self", panels(clusters, F32), specs, us=us)(
            *in_vmem(current, self_tiles), *others
        )

    def near_call(table, turned, given, *others):
        return call(
            functools.partial(near_kernel, len(given)),
            "near",
            (
                panels((columns - 1) * clusters, BF16),
                panels(clusters, BF16),
                panels((columns - 1) * clusters, F32),
                panels(clusters, F32),
            ),
            [SMEM_SPEC] + [VMEM_SPEC] * (1 + len(given)) + [ANY_SPEC] * len(others),
            [
                scratch(count * clusters, BF16),
                scratch(blocks, F32),
                scratch(count * clusters, F32),
            ],
            us=1.0,
        )(in_smem(table), *in_vmem(turned, *given), *others)

    gathered_coeffs = scratch(count * parents, BF16, 2 * rank)

    def far_call(table, messages):
        return call(
            functools.partial(far_kernel, len(messages), rows),
            "far",
            panels(clusters, F32),
            [SMEM_SPEC] + [VMEM_SPEC] * (3 + len(messages)),
            [gathered_coeffs],
            us=0.5,
        )(in_smem(table), *in_vmem(row_transfer, row_basis, coupling, *messages))

    def gather(message, *others):
        gathered = [message, to_sibling(message)]
        for x in across(message):
            gathered += [x, to_sibling(tie(x, *others) if others else x)]
        return gathered

    def both_to_sibling(send, send_own):
        arrived = to_sibling(jnp.concatenate([send, send_own]))
        return arrived[: send.shape[0]], arrived[send.shape[0] :]

    def all_coeffs(packed, crossed):
        beside = to_sibling(jnp.concatenate([packed, *crossed]))
        pieces = []
        for k, piece in enumerate([packed, *crossed]):
            pieces += [piece, beside[k * rows : (k + 1) * rows]]
        return pieces

    crossed = across(vectors)
    beside = to_sibling(vectors)
    packed, current, table = first_call(*in_hbm(*raw, vectors, column_basis, column_transfer))
    given = [current, beside]
    for x in crossed:
        given += [x, to_sibling(tie(x, packed))]
    crossed = across(packed)
    turned = turn_call(*in_vmem(near_tiles))
    send, send_own, keep, keep_own = near_call(table, turned, given, *crossed)
    arrived, arrived_own = to_sibling(send), to_sibling(send_own)
    pieces = all_coeffs(packed, crossed)

    if columns == 2 and ITERS == 2:
        both_out = (panels(clusters, BF16), panels(clusters, F32))
        other, other_sums = call(other_kernel, "other", both_out, [VMEM_SPEC] * 2, us=0.1)(
            *in_vmem(keep, arrived)
        )
        self_part = self_call(current, other)
        far_part = far_call(table, pieces)
        own, own_sums = call(
            own_kernel, "own", both_out, [VMEM_SPEC] * 4 + [ANY_SPEC], us=0.1
        )(*in_vmem(keep_own, arrived_own, self_part, far_part), other)

        def settled(sums, message, *others):
            specs = [VMEM_SPEC] * 2 + [ANY_SPEC] * len(others)
            return call(settle_kernel, "settle", panels(clusters, BF16), specs, us=0.1)(
                *in_vmem(sums, message), *others
            )

        other, own = to_column(other, 1), to_column(own, 1)
        current = settled(own_sums, other)
        beside = to_sibling(current)
        packed = coeffs_call(*in_vmem(current, column_basis, column_transfer))
        packed_column = to_column(packed, 1)
        column = settled(other_sums, own, packed, beside)
        given = [current, beside, column, to_sibling(column)]
        send, send_own, keep, keep_own = near_call(table, turned, given, packed)
        arrived, arrived_own = both_to_sibling(send, send_own)
        self_part = self_call(current, us=2.5)
        crossing = call(
            cross_kernel,
            "cross",
            panels(clusters, BF16),
            [VMEM_SPEC] * 2 + [ANY_SPEC] * 2,
            us=0.1,
        )(*in_vmem(keep, arrived), self_part, packed_column)
        far_part = far_call(table, all_coeffs(packed, [packed_column]))
        return call(last_kernel, "last", panels(clusters, BF16), [VMEM_SPEC] * 5, us=0.1)(
            *in_vmem(self_part, far_part, keep_own, arrived_own, to_column(crossing, 1))
        )

    self_part = self_call(current)
    far_part = far_call(table, pieces)

    def finished():
        near = keep_own + arrived_own.astype(F32)
        for s in range(1, columns):
            part = slice((s - 1) * clusters, s * clusters)
            partial = (keep[part] + arrived[part].astype(F32)).astype(BF16)
            near = near + to_column(partial, s).astype(F32)
        return (self_part + far_part + near).astype(BF16)

    for step in range(1, ITERS):
        message = call(
            message_kernel, "message", panels(clusters + rows, BF16), [VMEM_SPEC] * 3, us=0.5
        )(*in_vmem(finished(), column_basis, column_transfer))
        messages = gather(message)
        send, send_own, keep, keep_own = near_call(table, turned, messages)
        arrived, arrived_own = to_sibling(send), to_sibling(send_own)
        self_part = self_call(message)
        far_part = far_call(table, messages)
    return finished()


def solution(mesh):
    in_specs = (
        P(("groups", "loop"), "cuts", None),
        P(("groups", "loop"), None, None),
        P(("groups", "loop"), None, None),
        P(("groups", "loop"), None),
        P(("groups", "loop"), None),
        P(("groups", "loop"), None),
        P(("groups", "loop"), None, None),
        P(("groups", "loop"), None, None),
        P(("groups", "loop"), None, None),
        P(("groups", "loop"), None, None),
        P(("groups", "loop"), None, None),
        P(("groups", "loop"), None),
    )
    out_specs = P(("groups", "loop"), "cuts", None)
    return jax.shard_map(
        on_device, mesh=mesh, in_specs=in_specs, out_specs=out_specs, check_vma=False
    )
```

```python
import functools

import jax
import jax.numpy as jnp
from jax import lax
from jax.experimental import pallas as pl
from jax.experimental.pallas import tpu as pltpu
from jax.sharding import PartitionSpec as P

ITERS = 2
F32, BF16 = jnp.float32, jnp.bfloat16
ROWS_BY_ROWS = (((1,), (1,)), ((), ()))
ROWS_BY_COLUMNS = (((1,), (0,)), ((), ()))
VMEM_LIMIT = 8 * 1024 * 1024
FAR_ROW = 8


def dot(a, b, dims):
    return lax.dot_general(a, b, dims, preferred_element_type=F32)


def dot_wide(a, b, dims):
    rows = a.shape[0]
    upper = a.astype(BF16).astype(F32)
    halves = jnp.concatenate([upper, a - upper], axis=0).astype(BF16)
    both = dot(halves, b, dims)
    return both[:rows] + both[rows:]


def lanes_below(vectors, lanes):
    return lax.broadcasted_iota(jnp.int32, (vectors, lanes), 1) < lanes // 2


def load_all(sems, *pairs):
    copies = [pltpu.make_async_copy(x, y, sems.at[i]) for i, (x, y) in enumerate(pairs)]
    for copy in copies:
        copy.start()
    return copies


def parent_coeffs(current, column_basis, column_transfer, packed, first):
    clusters, rank, leaf_size = column_basis.shape
    vectors = current.shape[1]
    parents = clusters // 2
    lower = lanes_below(vectors, 2 * rank)
    leaves = []
    for p in range(parents):
        both = dot(
            current[2 * p : 2 * p + 2].reshape(2 * vectors, leaf_size),
            column_basis[2 * p : 2 * p + 2].reshape(2 * rank, leaf_size),
            ROWS_BY_ROWS,
        )
        leaves.append(jnp.where(lower, both[:vectors], both[vectors:]))
    totals = []
    for p in range(parents):
        transfer = column_transfer[2 * p : 2 * p + 2].reshape(2 * rank, rank)
        totals.append(dot_wide(leaves[p], transfer, ROWS_BY_COLUMNS))
    each = leaf_size // rank
    for p in range(0, parents, each):
        row = jnp.concatenate(totals[p : p + each], axis=-1)
        packed[first + p // each] = row.astype(BF16)


def unpack(packed, first, rows, rank, gathered, slot):
    for r in range(rows):
        row = packed[first + r].astype(F32)
        for k in range(row.shape[1] // (2 * rank)):
            pair = row[:, 2 * rank * k : 2 * rank * (k + 1)]
            lower = lanes_below(*pair.shape)
            turned = pltpu.roll(pair, rank, 1)
            gathered[slot] = jnp.where(lower, pair, turned).astype(BF16)
            gathered[slot + 1] = jnp.where(lower, turned, pair).astype(BF16)
            slot += 2
    return slot


def place_table(columns, clusters, source, target, local, far, values):
    me = lax.axis_index("loop")
    my_column = me // 2

    def around(shift):
        return jnp.where(shift < 0, shift + columns, shift)

    def other_core(home):
        return (home ^ me) & 1

    blocks = source.shape[1]
    home = source[...]
    shift = around(my_column - (home >> 1))
    values[0:1, :blocks] = (2 * shift + other_core(home)) * clusters + local[0:1]
    home = target[...]
    shift = around((home >> 1) - my_column)
    values[1:2, :blocks] = ((1 - other_core(home)) * columns + shift) * clusters + local[1:2]
    cluster = far[...]
    parents, far_count = cluster.shape
    home = jnp.zeros_like(cluster)
    for h in range(1, 2 * columns):
        home = home + jnp.where(cluster >= h * parents, 1, 0)
    shift = around(my_column - (home >> 1))
    place = (2 * shift + other_core(home)) * parents + cluster - home * parents
    values[FAR_ROW : FAR_ROW + parents, :far_count] = place


def first_kernel(
    columns,
    source_home,
    target_home,
    block_local,
    far_source,
    vectors,
    column_basis,
    column_transfer,
    packed,
    current,
    table,
    basis_held,
    transfer_held,
    source,
    target,
    local,
    far,
    values,
    sems,
):
    copies = load_all(
        sems,
        (source_home, source),
        (target_home, target),
        (block_local, local),
        (far_source, far),
        (vectors, current),
        (column_basis, basis_held),
        (column_transfer, transfer_held),
    )
    for copy in copies[:4]:
        copy.wait()
    place_table(columns, vectors.shape[0], source, target, local, far, values)
    placed = pltpu.make_async_copy(values, table, sems.at[7])
    placed.start()
    for copy in copies[4:]:
        copy.wait()
    parent_coeffs(current, basis_held, transfer_held, packed, 0)
    placed.wait()


def coeffs_kernel(current, column_basis, column_transfer, packed):
    parent_coeffs(current, column_basis, column_transfer, packed, 0)


def message_kernel(current, column_basis, column_transfer, message):
    clusters = current.shape[0]
    message[:clusters] = current[...]
    parent_coeffs(current, column_basis, column_transfer, message, clusters)


def self_kernel(current, self_tiles, *others):
    self_part = others[-1]
    for c in range(self_part.shape[0]):
        self_part[c] = dot(current[c], self_tiles[c], ROWS_BY_ROWS)


def turn_kernel(tiles, turned):
    for b in range(tiles.shape[0]):
        turned[b] = tiles[b].T


def near_kernel(panel_count, table, tiles, *refs):
    panels, refs = refs[:panel_count], refs[panel_count:]
    send, send_own, keep, keep_own, gathered, products, sums = refs[-7:]
    each = gathered.shape[0] // panel_count
    for k, panel in enumerate(panels):
        gathered[k * each : (k + 1) * each] = panel[:each]
    sums[...] = jnp.zeros_like(sums)
    blocks = tiles.shape[0]
    for b in range(blocks):
        products[b] = dot(gathered[table[0, b]], tiles[b], ROWS_BY_COLUMNS)
    for b in range(blocks):
        sums[table[1, b]] += products[b]
    own, half = keep_own.shape[0], sums.shape[0] // 2
    send_own[...] = sums[:own].astype(BF16)
    send[...] = sums[own:half].astype(BF16)
    keep_own[...] = sums[half : half + own]
    keep[...] = sums[half + own :]


def near_half(half, table, tiles, gathered, send, keep, products, sums):
    lanes = send.shape[2]
    sums[...] = jnp.zeros_like(sums)
    blocks = tiles.shape[0]
    for b in range(blocks):
        tile = tiles[b, :, half * lanes : (half + 1) * lanes]
        products[b] = dot(gathered[table[0, b]], tile, ROWS_BY_COLUMNS)
    for b in range(blocks):
        sums[table[1, b]] += products[b]
    middle = send.shape[0]
    send[...] = sums[:middle].astype(BF16)
    keep[...] = sums[middle:]


def first_half_kernel(panel_count, table, tiles, *refs):
    panels, (send, keep, gathered, products, sums) = refs[:panel_count], refs[-5:]
    each = gathered.shape[0] // panel_count
    for k, panel in enumerate(panels):
        gathered[k * each : (k + 1) * each] = panel[:each]
    near_half(0, table, tiles, gathered, send, keep, products, sums)


def second_half_kernel(table, tiles, gathered, send, keep, products, sums):
    near_half(1, table, tiles, gathered, send, keep, products, sums)


def far_products(table, row_transfer, row_basis, coupling, gathered, store):
    vectors, lanes = gathered.shape[1:]
    rank, leaf_size = row_basis.shape[1:]
    parents = coupling.shape[0]
    far_count = coupling.shape[2] // rank
    lower = lanes_below(vectors, lanes)
    parent_outs = []
    for p in range(parents):
        pairs = []
        for f in range(0, far_count, 2):
            first = gathered[table[FAR_ROW + p, f]]
            second = gathered[table[FAR_ROW + p, f + 1]]
            pairs.append(jnp.where(lower, first.astype(F32), second.astype(F32)).astype(BF16))
        parent_outs.append(dot(jnp.concatenate(pairs, axis=-1), coupling[p], ROWS_BY_ROWS))
    leaf_outs = []
    for p in range(parents):
        transfer = jnp.concatenate([row_transfer[2 * p], row_transfer[2 * p + 1]], axis=-1)
        leaf_outs.append(dot_wide(parent_outs[p], transfer, ROWS_BY_COLUMNS))
    for p in range(parents):
        zero = jnp.zeros_like(leaf_outs[p])
        stacked = jnp.concatenate(
            [jnp.where(lower, leaf_outs[p], zero), jnp.where(lower, zero, leaf_outs[p])], axis=0
        ).astype(BF16)
        basis = row_basis[2 * p : 2 * p + 2].reshape(2 * rank, leaf_size)
        both = dot(stacked, basis, ROWS_BY_COLUMNS)
        store(2 * p, both.reshape(2, vectors, leaf_size))


def far_kernel(message_count, rows, table, row_transfer, row_basis, coupling, *refs):
    messages, (far_part, gathered) = refs[:message_count], refs[-2:]
    slot = 0
    for message in messages:
        slot = unpack(message, message.shape[0] - rows, rows, row_basis.shape[1], gathered, slot)

    def store(c, both):
        far_part[c : c + 2] = both

    far_products(table, row_transfer, row_basis, coupling, gathered, store)


def other_kernel(keep, arrived, message, sums):
    other = keep[...] + arrived[...].astype(F32)
    sums[...] = other
    message[...] = other.astype(BF16)


def own_kernel(keep, arrived, self_part, far_part, sent_before, message, sums):
    own = keep[...] + arrived[...].astype(F32) + self_part[...] + far_part[...]
    sums[...] = own
    message[...] = own.astype(BF16)


def settle_kernel(sums, message, *others):
    current = others[-1]
    current[...] = (sums[...] + message[...].astype(F32)).astype(BF16)


def cross_kernel(keep, arrived, *refs):
    message = refs[-1]
    half = message.shape[0]
    message[...] = (keep[half:] + arrived[half:].astype(F32)).astype(BF16)


def last_kernel(*refs):
    keep, arrived, crossed, (self_part, far_part, product) = (
        refs[:2], refs[2:4], refs[4:6], refs[6:]
    )
    count = product.shape[0]
    halves = [
        k[:count] + a[:count].astype(F32) + x[...].astype(F32)
        for k, a, x in zip(keep, arrived, crossed)
    ]
    near = jnp.concatenate(halves, axis=-1)
    product[...] = (self_part[...] + far_part[...] + near).astype(BF16)


def tie_kernel(*refs):
    pass


def in_vmem(*arrays):
    return [pltpu.with_memory_space_constraint(a, pltpu.VMEM) for a in arrays]


def in_hbm(*arrays):
    return [pltpu.with_memory_space_constraint(a, pltpu.HBM) for a in arrays]


def in_smem(array):
    return pltpu.with_memory_space_constraint(array, pltpu.SMEM)


VMEM_SPEC = pl.BlockSpec(memory_space=pltpu.VMEM)
HBM_SPEC = pl.BlockSpec(memory_space=pltpu.HBM)
ANY_SPEC = pl.BlockSpec(memory_space=pl.ANY)
SMEM_SPEC = pl.BlockSpec(memory_space=pltpu.SMEM)


def call(kernel, name, out_shape, in_specs, scratch_shapes=(), out_specs=None, us=1.0):
    return pl.pallas_call(
        kernel,
        name=name,
        out_shape=out_shape,
        in_specs=in_specs,
        out_specs=jax.tree.map(lambda _: VMEM_SPEC, out_shape) if out_specs is None else out_specs,
        scratch_shapes=scratch_shapes,
        compiler_params=pltpu.CompilerParams(vmem_limit_bytes=VMEM_LIMIT),
        cost_estimate=pl.CostEstimate(
            flops=int(us * 1.0e9), bytes_accessed=0, transcendentals=0
        ),
    )


def tie(x, *others):
    return pl.pallas_call(
        tie_kernel,
        name="tie",
        out_shape=pltpu.VMEM(x.shape, x.dtype),
        in_specs=[VMEM_SPEC] + [ANY_SPEC] * len(others),
        out_specs=VMEM_SPEC,
        input_output_aliases={0: 0},
        compiler_params=pltpu.CompilerParams(vmem_limit_bytes=VMEM_LIMIT),
    )(*in_vmem(x), *others)


def on_device(
    vectors,
    near_tiles,
    self_tiles,
    source_home,
    target_home,
    block_local,
    column_basis,
    row_basis,
    column_transfer,
    row_transfer,
    coupling,
    far_source,
):
    clusters, vector_count, leaf_size = vectors.shape
    blocks = near_tiles.shape[0]
    rank = column_basis.shape[1]
    parents, far_count = far_source.shape
    count = lax.axis_size("loop")
    columns = count // 2
    sibling = [(i, i ^ 1) for i in range(count)]

    def to_sibling(x):
        return lax.ppermute(x, "loop", sibling)

    def to_column(x, shift):
        return lax.ppermute(x, "loop", [(i, (i + 2 * shift) % count) for i in range(count)])

    def across(x):
        return [to_column(x, shift) for shift in range(1, columns)]

    def panels(number, dtype, width=leaf_size):
        return jax.ShapeDtypeStruct((number, vector_count, width), dtype)

    def scratch(number, dtype, width=leaf_size):
        return pltpu.VMEM((number, vector_count, width), dtype)

    rows = parents * rank // leaf_size
    raw = (source_home.T, target_home.T, block_local.T, far_source)
    table_shape = (FAR_ROW + parents, 128)
    first_call = call(
        functools.partial(first_kernel, columns),
        "first",
        (
            panels(rows, BF16),
            pltpu.VMEM(vectors.shape, BF16),
            pltpu.SMEM(table_shape, jnp.int32),
        ),
        [HBM_SPEC] * 7,
        [pltpu.VMEM(x.shape, x.dtype) for x in (column_basis, column_transfer, *raw)]
        + [pltpu.VMEM(table_shape, jnp.int32), pltpu.SemaphoreType.DMA((8,))],
        out_specs=(VMEM_SPEC, VMEM_SPEC, SMEM_SPEC),
        us=10.0,
    )
    turn_call = call(
        turn_kernel, "turn", pltpu.VMEM(near_tiles.shape, BF16), [VMEM_SPEC], us=2.5
    )
    coeffs_call = call(coeffs_kernel, "coeffs", panels(rows, BF16), [VMEM_SPEC] * 3, us=0.5)
    def self_call(current, *others, us=0.6):
        specs = [VMEM_SPEC] * 2 + [ANY_SPEC] * len(others)
        return call(self_kernel, "self", panels(clusters, F32), specs, us=us)(
            *in_vmem(current, self_tiles), *others
        )

    def near_call(table, turned, given, *others):
        return call(
            functools.partial(near_kernel, len(given)),
            "near",
            (
                panels((columns - 1) * clusters, BF16),
                panels(clusters, BF16),
                panels((columns - 1) * clusters, F32),
                panels(clusters, F32),
            ),
            [SMEM_SPEC] + [VMEM_SPEC] * (1 + len(given)) + [ANY_SPEC] * len(others),
            [
                scratch(count * clusters, BF16),
                scratch(blocks, F32),
                scratch(count * clusters, F32),
            ],
            us=1.0,
        )(in_smem(table), *in_vmem(turned, *given), *others)

    half_size = leaf_size // 2

    def half_calls(table, turned, given):
        outs = (
            panels(columns * clusters, BF16, half_size),
            panels(columns * clusters, F32, half_size),
        )
        scratches = [scratch(blocks, F32, half_size), scratch(count * clusters, F32, half_size)]
        send, keep, gathered = call(
            functools.partial(first_half_kernel, len(given)),
            "first_half",
            (*outs, scratch(count * clusters, BF16)),
            [SMEM_SPEC] + [VMEM_SPEC] * (1 + len(given)),
            scratches,
            us=0.5,
        )(in_smem(table), *in_vmem(turned, *given))
        next_send, next_keep = call(
            second_half_kernel, "second_half", outs, [SMEM_SPEC] + [VMEM_SPEC] * 2, scratches, us=0.5
        )(in_smem(table), *in_vmem(turned, gathered))
        arrived = (to_sibling(send), to_sibling(next_send))
        return (keep, next_keep), arrived

    gathered_coeffs = scratch(count * parents, BF16, 2 * rank)

    def far_call(table, messages):
        return call(
            functools.partial(far_kernel, len(messages), rows),
            "far",
            panels(clusters, F32),
            [SMEM_SPEC] + [VMEM_SPEC] * (3 + len(messages)),
            [gathered_coeffs],
            us=0.5,
        )(in_smem(table), *in_vmem(row_transfer, row_basis, coupling, *messages))

    def gather(message, *others):
        gathered = [message, to_sibling(message)]
        for x in across(message):
            gathered += [x, to_sibling(tie(x, *others) if others else x)]
        return gathered

    def all_coeffs(packed, crossed):
        beside = to_sibling(jnp.concatenate([packed, *crossed]))
        pieces = []
        for k, piece in enumerate([packed, *crossed]):
            pieces += [piece, beside[k * rows : (k + 1) * rows]]
        return pieces

    crossed = across(vectors)
    packed, current, table = first_call(*in_hbm(*raw, vectors, column_basis, column_transfer))
    given = [current, to_sibling(current)]
    for x in crossed:
        given += [x, to_sibling(tie(x, packed))]
    crossed = across(packed)
    turned = turn_call(*in_vmem(near_tiles))
    send, send_own, keep, keep_own = near_call(table, turned, given, *crossed)
    arrived, arrived_own = to_sibling(send), to_sibling(send_own)
    pieces = all_coeffs(packed, crossed)

    if columns == 2 and ITERS == 2:
        both_out = (panels(clusters, BF16), panels(clusters, F32))
        other, other_sums = call(other_kernel, "other", both_out, [VMEM_SPEC] * 2, us=0.1)(
            *in_vmem(keep, arrived)
        )
        self_part = self_call(current, other)
        far_part = far_call(table, pieces)
        own, own_sums = call(
            own_kernel, "own", both_out, [VMEM_SPEC] * 4 + [ANY_SPEC], us=0.1
        )(*in_vmem(keep_own, arrived_own, self_part, far_part), other)

        def settled(sums, message, *others):
            specs = [VMEM_SPEC] * 2 + [ANY_SPEC] * len(others)
            return call(settle_kernel, "settle", panels(clusters, BF16), specs, us=0.1)(
                *in_vmem(sums, message), *others
            )

        other, own = to_column(other, 1), to_column(own, 1)
        current = settled(own_sums, other)
        beside = to_sibling(current)
        packed = coeffs_call(*in_vmem(current, column_basis, column_transfer))
        packed_column = to_column(packed, 1)
        column = settled(other_sums, own, packed, beside)
        given = [current, beside, column, to_sibling(column)]
        keep, arrived = half_calls(table, turned, given)
        self_part = self_call(current, us=2.5)
        crossing = []
        for one_keep, one_arrived, first in zip(keep, arrived, ((self_part,), (self_part, packed_column))):
            others = (*first, *crossing)
            crossing.append(
                call(
                    cross_kernel,
                    "cross",
                    panels(clusters, BF16, half_size),
                    [VMEM_SPEC] * 2 + [ANY_SPEC] * len(others),
                    us=1.0,
                )(*in_vmem(one_keep, one_arrived), *others)
            )
        far_part = far_call(table, all_coeffs(packed, [packed_column]))
        return call(last_kernel, "last", panels(clusters, BF16), [VMEM_SPEC] * 8, us=0.1)(
            *in_vmem(*keep, *arrived, *(to_column(x, 1) for x in crossing), self_part, far_part)
        )

    self_part = self_call(current)
    far_part = far_call(table, pieces)

    def finished():
        near = keep_own + arrived_own.astype(F32)
        for s in range(1, columns):
            part = slice((s - 1) * clusters, s * clusters)
            partial = (keep[part] + arrived[part].astype(F32)).astype(BF16)
            near = near + to_column(partial, s).astype(F32)
        return (self_part + far_part + near).astype(BF16)

    for step in range(1, ITERS):
        message = call(
            message_kernel, "message", panels(clusters + rows, BF16), [VMEM_SPEC] * 3, us=0.5
        )(*in_vmem(finished(), column_basis, column_transfer))
        messages = gather(message)
        send, send_own, keep, keep_own = near_call(table, turned, messages)
        arrived, arrived_own = to_sibling(send), to_sibling(send_own)
        self_part = self_call(message)
        far_part = far_call(table, messages)
    return finished()


def solution(mesh):
    in_specs = (
        P(("groups", "loop"), "cuts", None),
        P(("groups", "loop"), None, None),
        P(("groups", "loop"), None, None),
        P(("groups", "loop"), None),
        P(("groups", "loop"), None),
        P(("groups", "loop"), None),
        P(("groups", "loop"), None, None),
        P(("groups", "loop"), None, None),
        P(("groups", "loop"), None, None),
        P(("groups", "loop"), None, None),
        P(("groups", "loop"), None, None),
        P(("groups", "loop"), None),
    )
    out_specs = P(("groups", "loop"), "cuts", None)
    return jax.shard_map(
        on_device, mesh=mesh, in_specs=in_specs, out_specs=out_specs, check_vma=False
    )
```

```python
import functools

import jax
import jax.numpy as jnp
from jax import lax
from jax.experimental import pallas as pl
from jax.experimental.pallas import tpu as pltpu
from jax.sharding import PartitionSpec as P

ITERS = 2
F32, BF16 = jnp.float32, jnp.bfloat16
ROWS_BY_ROWS = (((1,), (1,)), ((), ()))
ROWS_BY_COLUMNS = (((1,), (0,)), ((), ()))
VMEM_LIMIT = 8 * 1024 * 1024
FAR_ROW = 8


def dot(a, b, dims):
    return lax.dot_general(a, b, dims, preferred_element_type=F32)


def dot_wide(a, b, dims):
    rows = a.shape[0]
    upper = a.astype(BF16).astype(F32)
    halves = jnp.concatenate([upper, a - upper], axis=0).astype(BF16)
    both = dot(halves, b, dims)
    return both[:rows] + both[rows:]


def lanes_below(vectors, lanes):
    return lax.broadcasted_iota(jnp.int32, (vectors, lanes), 1) < lanes // 2


def load_all(sems, *pairs):
    copies = [pltpu.make_async_copy(x, y, sems.at[i]) for i, (x, y) in enumerate(pairs)]
    for copy in copies:
        copy.start()
    return copies


def parent_coeffs(current, column_basis, column_transfer, packed, first):
    clusters, rank, leaf_size = column_basis.shape
    vectors = current.shape[1]
    parents = clusters // 2
    lower = lanes_below(vectors, 2 * rank)
    leaves = []
    for p in range(parents):
        both = dot(
            current[2 * p : 2 * p + 2].reshape(2 * vectors, leaf_size),
            column_basis[2 * p : 2 * p + 2].reshape(2 * rank, leaf_size),
            ROWS_BY_ROWS,
        )
        leaves.append(jnp.where(lower, both[:vectors], both[vectors:]))
    totals = []
    for p in range(parents):
        transfer = column_transfer[2 * p : 2 * p + 2].reshape(2 * rank, rank)
        totals.append(dot_wide(leaves[p], transfer, ROWS_BY_COLUMNS))
    each = leaf_size // rank
    for p in range(0, parents, each):
        row = jnp.concatenate(totals[p : p + each], axis=-1)
        packed[first + p // each] = row.astype(BF16)


def unpack(packed, first, rows, rank, gathered, slot):
    for r in range(rows):
        row = packed[first + r].astype(F32)
        for k in range(row.shape[1] // (2 * rank)):
            pair = row[:, 2 * rank * k : 2 * rank * (k + 1)]
            lower = lanes_below(*pair.shape)
            turned = pltpu.roll(pair, rank, 1)
            gathered[slot] = jnp.where(lower, pair, turned).astype(BF16)
            gathered[slot + 1] = jnp.where(lower, turned, pair).astype(BF16)
            slot += 2
    return slot


def place_table(columns, clusters, source, target, local, far, values, places):
    me = lax.axis_index("loop")
    my_column = me // 2

    def around(shift):
        return jnp.where(shift < 0, shift + columns, shift)

    def other_core(home):
        return (home ^ me) & 1

    blocks = source.shape[1]
    home = source[...]
    shift = around(my_column - (home >> 1))
    values[0:1, :blocks] = (2 * shift + other_core(home)) * clusters + local[0:1]
    home = target[...]
    shift = around((home >> 1) - my_column)
    values[1:2, :blocks] = ((1 - other_core(home)) * columns + shift) * clusters + local[1:2]
    cluster = far[...]
    parents, far_count = cluster.shape
    home = jnp.zeros_like(cluster)
    for h in range(1, 2 * columns):
        home = home + jnp.where(cluster >= h * parents, 1, 0)
    shift = around(my_column - (home >> 1))
    place = (2 * shift + other_core(home)) * parents + cluster - home * parents
    values[FAR_ROW : FAR_ROW + parents, :far_count] = place
    home = source[...]
    shift = around(my_column - (home >> 1))
    places[0:1, :blocks] = (2 * shift + (home & 1)) * clusters + local[0:1]
    home = target[...]
    shift = around((home >> 1) - my_column)
    places[1:2, :blocks] = (2 * shift + (home & 1)) * clusters + local[1:2]


def first_kernel(
    columns,
    source_home,
    target_home,
    block_local,
    far_source,
    vectors,
    column_basis,
    column_transfer,
    packed,
    current,
    places,
    table,
    basis_held,
    transfer_held,
    source,
    target,
    local,
    far,
    values,
    sems,
):
    copies = load_all(
        sems,
        (source_home, source),
        (target_home, target),
        (block_local, local),
        (far_source, far),
        (vectors, current),
        (column_basis, basis_held),
        (column_transfer, transfer_held),
    )
    for copy in copies[:4]:
        copy.wait()
    place_table(columns, vectors.shape[0], source, target, local, far, values, places)
    placed = pltpu.make_async_copy(values, table, sems.at[7])
    placed.start()
    for copy in copies[4:]:
        copy.wait()
    parent_coeffs(current, basis_held, transfer_held, packed, 0)
    placed.wait()


def coeffs_kernel(current, column_basis, column_transfer, packed):
    parent_coeffs(current, column_basis, column_transfer, packed, 0)


def message_kernel(current, column_basis, column_transfer, message):
    clusters = current.shape[0]
    message[:clusters] = current[...]
    parent_coeffs(current, column_basis, column_transfer, message, clusters)


def self_kernel(current, self_tiles, *others):
    self_part = others[-1]
    for c in range(self_part.shape[0]):
        self_part[c] = dot(current[c], self_tiles[c], ROWS_BY_ROWS)


def turn_kernel(tiles, mine, theirs):
    lanes = mine.shape[2]
    core = lax.axis_index("loop") % 2
    start = pl.multiple_of(core * lanes, lanes)
    other = pl.multiple_of((1 - core) * lanes, lanes)
    for b in range(tiles.shape[0]):
        mine[b] = tiles[b, pl.ds(start, lanes), :].T
        theirs[b] = tiles[b, pl.ds(other, lanes), :].T


def near_kernel(panel_count, packed_count, table, mine, theirs, *refs):
    panels, refs = refs[:panel_count], refs[panel_count:]
    packed = refs[:packed_count]
    send, send_own, keep, keep_own, gathered, products, sums = refs[-7:]
    each = gathered.shape[0] // panel_count
    for k, panel in enumerate(panels):
        gathered[k * each : (k + 1) * each] = panel[:each]
    sums[...] = jnp.zeros_like(sums)
    blocks = mine.shape[0]
    for b in range(blocks):
        tile = jnp.concatenate([mine[b], theirs[b]], axis=-1)
        products[b] = dot(gathered[table[0, b]], tile, ROWS_BY_COLUMNS)
    for b in range(blocks):
        sums[table[1, b]] += products[b]
    own, half = keep_own.shape[0], sums.shape[0] // 2
    core = lax.axis_index("loop") % 2

    def in_order(x):
        lanes = x.shape[-1] // 2
        here, beside = x[..., :lanes], x[..., lanes:]
        return jnp.concatenate(
            [jnp.where(core == 0, here, beside), jnp.where(core == 0, beside, here)], axis=-1
        )

    send_own[:own] = in_order(sums[:own]).astype(BF16)
    for k, coeffs in enumerate(packed):
        rows = coeffs.shape[0]
        send_own[own + k * rows : own + (k + 1) * rows] = coeffs[...]
    send[...] = in_order(sums[own:half]).astype(BF16)
    keep_own[...] = in_order(sums[half : half + own])
    keep[...] = in_order(sums[half + own :])


def first_self_kernel(
    current, self_tiles, places, places_beside, sent_before, self_part, table, sems
):
    copies = load_all(
        sems,
        (places, table.at[pl.ds(0, FAR_ROW)]),
        (places_beside, table.at[pl.ds(FAR_ROW, FAR_ROW)]),
    )
    self_kernel(current, self_tiles, self_part)
    for copy in copies:
        copy.wait()


def half_kernel(
    table,
    mine,
    beside,
    current,
    current_beside,
    column,
    column_beside,
    across,
    diagonal,
    send,
    keep,
    gathered,
    products,
    sums,
):
    clusters = current.shape[0]
    core = lax.axis_index("loop") % 2

    def at(slot):
        return pl.ds(slot * clusters, clusters)

    gathered[at(core)] = current[...]
    gathered[at(1 - core)] = current_beside[...]
    gathered[at(2 + core)] = column[...]
    gathered[at(3 - core)] = column_beside[...]
    sums[...] = jnp.zeros_like(sums)
    blocks = mine.shape[0]
    for k, tiles in enumerate((mine, beside)):
        for b in range(blocks):
            source = table[k * FAR_ROW, b]
            products[k * blocks + b] = dot(gathered[source], tiles[b], ROWS_BY_COLUMNS)
    for k in range(2):
        for b in range(blocks):
            sums[table[k * FAR_ROW + 1, b]] += products[k * blocks + b]
    across[...] = sums[at(2 + core)].astype(BF16)
    diagonal[...] = sums[at(3 - core)].astype(BF16)
    send[...] = sums[at(1 - core)].astype(BF16)
    keep[...] = sums[at(core)]


def far_products(table, row_transfer, row_basis, coupling, gathered, store):
    vectors, lanes = gathered.shape[1:]
    rank, leaf_size = row_basis.shape[1:]
    parents = coupling.shape[0]
    far_count = coupling.shape[2] // rank
    lower = lanes_below(vectors, lanes)
    parent_outs = []
    for p in range(parents):
        pairs = []
        for f in range(0, far_count, 2):
            first = gathered[table[FAR_ROW + p, f]]
            second = gathered[table[FAR_ROW + p, f + 1]]
            pairs.append(jnp.where(lower, first.astype(F32), second.astype(F32)).astype(BF16))
        parent_outs.append(dot(jnp.concatenate(pairs, axis=-1), coupling[p], ROWS_BY_ROWS))
    leaf_outs = []
    for p in range(parents):
        transfer = jnp.concatenate([row_transfer[2 * p], row_transfer[2 * p + 1]], axis=-1)
        leaf_outs.append(dot_wide(parent_outs[p], transfer, ROWS_BY_COLUMNS))
    for p in range(parents):
        zero = jnp.zeros_like(leaf_outs[p])
        stacked = jnp.concatenate(
            [jnp.where(lower, leaf_outs[p], zero), jnp.where(lower, zero, leaf_outs[p])], axis=0
        ).astype(BF16)
        basis = row_basis[2 * p : 2 * p + 2].reshape(2 * rank, leaf_size)
        both = dot(stacked, basis, ROWS_BY_COLUMNS)
        store(2 * p, both.reshape(2, vectors, leaf_size))


def far_kernel(starts, rows, table, row_transfer, row_basis, coupling, *refs):
    messages, (far_part, gathered) = refs[: len(starts)], refs[-2:]
    slot = 0
    for message, start in zip(messages, starts):
        slot = unpack(message, start, rows, row_basis.shape[1], gathered, slot)

    def store(c, both):
        far_part[c : c + 2] = both

    far_products(table, row_transfer, row_basis, coupling, gathered, store)


def other_kernel(keep, arrived, message, sums):
    other = keep[...] + arrived[...].astype(F32)
    sums[...] = other
    message[...] = other.astype(BF16)


def own_kernel(keep, arrived, self_part, far_part, sent_before, message, sums):
    near = keep[...] + arrived[: keep.shape[0]].astype(F32)
    own = near + self_part[...] + far_part[...]
    sums[...] = own
    message[...] = own.astype(BF16)


def settle_kernel(sums, message, *others):
    current = others[-1]
    current[...] = (sums[...] + message[...].astype(F32)).astype(BF16)


def last_kernel(self_part, far_part, keep, crossed, arrived, diagonal, product):
    core = lax.axis_index("loop") % 2
    here = keep[...] + crossed[...].astype(F32)
    beside = arrived[...].astype(F32) + diagonal[...].astype(F32)
    near = jnp.concatenate(
        [jnp.where(core == 0, here, beside), jnp.where(core == 0, beside, here)], axis=-1
    )
    product[...] = (self_part[...] + far_part[...] + near).astype(BF16)


def tie_kernel(*refs):
    pass


def in_vmem(*arrays):
    return [pltpu.with_memory_space_constraint(a, pltpu.VMEM) for a in arrays]


def in_hbm(*arrays):
    return [pltpu.with_memory_space_constraint(a, pltpu.HBM) for a in arrays]


def in_smem(array):
    return pltpu.with_memory_space_constraint(array, pltpu.SMEM)


VMEM_SPEC = pl.BlockSpec(memory_space=pltpu.VMEM)
HBM_SPEC = pl.BlockSpec(memory_space=pltpu.HBM)
ANY_SPEC = pl.BlockSpec(memory_space=pl.ANY)
SMEM_SPEC = pl.BlockSpec(memory_space=pltpu.SMEM)


def call(kernel, name, out_shape, in_specs, scratch_shapes=(), out_specs=None, us=1.0):
    return pl.pallas_call(
        kernel,
        name=name,
        out_shape=out_shape,
        in_specs=in_specs,
        out_specs=jax.tree.map(lambda _: VMEM_SPEC, out_shape) if out_specs is None else out_specs,
        scratch_shapes=scratch_shapes,
        compiler_params=pltpu.CompilerParams(vmem_limit_bytes=VMEM_LIMIT),
        cost_estimate=pl.CostEstimate(
            flops=int(us * 1.0e9), bytes_accessed=0, transcendentals=0
        ),
    )


def tie(x, *others, us=0.0):
    return pl.pallas_call(
        tie_kernel,
        name="tie",
        out_shape=pltpu.VMEM(x.shape, x.dtype),
        in_specs=[VMEM_SPEC] + [ANY_SPEC] * len(others),
        out_specs=VMEM_SPEC,
        input_output_aliases={0: 0},
        compiler_params=pltpu.CompilerParams(vmem_limit_bytes=VMEM_LIMIT),
        cost_estimate=pl.CostEstimate(
            flops=int(us * 1.0e9), bytes_accessed=0, transcendentals=0
        ),
    )(*in_vmem(x), *others)


def on_device(
    vectors,
    near_tiles,
    self_tiles,
    source_home,
    target_home,
    block_local,
    column_basis,
    row_basis,
    column_transfer,
    row_transfer,
    coupling,
    far_source,
):
    clusters, vector_count, leaf_size = vectors.shape
    blocks = near_tiles.shape[0]
    rank = column_basis.shape[1]
    parents, far_count = far_source.shape
    count = lax.axis_size("loop")
    columns = count // 2
    sibling = [(i, i ^ 1) for i in range(count)]

    def to_sibling(x):
        return lax.ppermute(x, "loop", sibling)

    def to_column(x, shift):
        return lax.ppermute(x, "loop", [(i, (i + 2 * shift) % count) for i in range(count)])

    def across(x):
        return [to_column(x, shift) for shift in range(1, columns)]

    def panels(number, dtype, width=leaf_size):
        return jax.ShapeDtypeStruct((number, vector_count, width), dtype)

    def scratch(number, dtype, width=leaf_size):
        return pltpu.VMEM((number, vector_count, width), dtype)

    rows = parents * rank // leaf_size
    raw = (source_home.T, target_home.T, block_local.T, far_source)
    table_shape = (FAR_ROW + parents, 128)
    first_call = call(
        functools.partial(first_kernel, columns),
        "first",
        (
            panels(rows, BF16),
            pltpu.VMEM(vectors.shape, BF16),
            pltpu.VMEM((FAR_ROW, 128), jnp.int32),
            pltpu.SMEM(table_shape, jnp.int32),
        ),
        [HBM_SPEC] * 7,
        [pltpu.VMEM(x.shape, x.dtype) for x in (column_basis, column_transfer, *raw)]
        + [pltpu.VMEM(table_shape, jnp.int32), pltpu.SemaphoreType.DMA((8,))],
        out_specs=(VMEM_SPEC, VMEM_SPEC, VMEM_SPEC, SMEM_SPEC),
        us=10.0,
    )
    half_tiles = pltpu.VMEM((blocks, leaf_size, leaf_size // 2), BF16)
    turn_call = call(turn_kernel, "turn", (half_tiles, half_tiles), [VMEM_SPEC], us=2.5)
    coeffs_call = call(coeffs_kernel, "coeffs", panels(rows, BF16), [VMEM_SPEC] * 3, us=0.5)
    def self_call(current, *others, us=0.6):
        specs = [VMEM_SPEC] * 2 + [ANY_SPEC] * len(others)
        return call(self_kernel, "self", panels(clusters, F32), specs, us=us)(
            *in_vmem(current, self_tiles), *others
        )

    def near_call(table, given, packed=()):
        return call(
            functools.partial(near_kernel, len(given), len(packed)),
            "near",
            (
                panels((columns - 1) * clusters, BF16),
                panels(clusters + len(packed) * rows, BF16),
                panels((columns - 1) * clusters, F32),
                panels(clusters, F32),
            ),
            [SMEM_SPEC] + [VMEM_SPEC] * (2 + len(given) + len(packed)),
            [
                scratch(count * clusters, BF16),
                scratch(blocks, F32),
                scratch(count * clusters, F32),
            ],
            us=1.0,
        )(in_smem(table), *in_vmem(mine, theirs, *given, *packed))

    half_size = leaf_size // 2
    first_self_call = call(
        first_self_kernel,
        "first_self",
        (panels(clusters, F32), pltpu.SMEM((2 * FAR_ROW, 128), jnp.int32)),
        [VMEM_SPEC] * 4 + [ANY_SPEC],
        [pltpu.SemaphoreType.DMA((2,))],
        out_specs=(VMEM_SPEC, SMEM_SPEC),
        us=0.6,
    )
    half_call = call(
        half_kernel,
        "half",
        (*(panels(clusters, BF16, half_size),) * 3, panels(clusters, F32, half_size)),
        [SMEM_SPEC] + [VMEM_SPEC] * 6,
        [
            scratch(count * clusters, BF16),
            scratch(2 * blocks, F32, half_size),
            scratch(count * clusters, F32, half_size),
        ],
        us=1.0,
    )

    gathered_coeffs = scratch(count * parents, BF16, 2 * rank)

    def far_call(table, messages, starts=None):
        if starts is None:
            starts = [x.shape[0] - rows for x in messages]
        return call(
            functools.partial(far_kernel, tuple(starts), rows),
            "far",
            panels(clusters, F32),
            [SMEM_SPEC] + [VMEM_SPEC] * (3 + len(messages)),
            [gathered_coeffs],
            us=0.5,
        )(in_smem(table), *in_vmem(row_transfer, row_basis, coupling, *messages))

    def gather(message, *others):
        gathered = [message, to_sibling(message)]
        for x in across(message):
            gathered += [x, to_sibling(tie(x, *others) if others else x)]
        return gathered

    def all_coeffs(packed, crossed):
        beside = to_sibling(jnp.concatenate([packed, *crossed]))
        pieces = []
        for k, piece in enumerate([packed, *crossed]):
            pieces += [piece, beside[k * rows : (k + 1) * rows]]
        return pieces

    crossed = across(vectors)
    packed, current, places, table = first_call(*in_hbm(*raw, vectors, column_basis, column_transfer))
    places_beside = to_sibling(places)
    given = [current, to_sibling(current)]
    for x in crossed:
        given += [x, to_sibling(tie(x, packed, places_beside))]
    crossed = across(packed)
    mine, theirs = turn_call(*in_vmem(near_tiles))
    send, send_own, keep, keep_own = near_call(table, given, [packed, *crossed])
    arrived, arrived_own = to_sibling(send), to_sibling(send_own)
    pieces, starts = [], []
    for k, piece in enumerate([packed, *crossed]):
        pieces += [piece, arrived_own]
        starts += [0, clusters + k * rows]

    if columns == 2 and ITERS == 2:
        both_out = (panels(clusters, BF16), panels(clusters, F32))
        other, other_sums = call(other_kernel, "other", both_out, [VMEM_SPEC] * 2, us=0.1)(
            *in_vmem(keep, arrived)
        )
        far_part = far_call(table, pieces, starts)
        self_part, both_places = first_self_call(
            *in_vmem(current, self_tiles, places, places_beside), other
        )
        theirs = to_sibling(tie(theirs, other,arrived_own, places_beside))
        own, own_sums = call(
            own_kernel, "own", both_out, [VMEM_SPEC] * 4 + [ANY_SPEC], us=0.1
        )(*in_vmem(keep_own, arrived_own, self_part, far_part), other)

        def settled(sums, message, *others):
            specs = [VMEM_SPEC] * 2 + [ANY_SPEC] * len(others)
            return call(settle_kernel, "settle", panels(clusters, BF16), specs, us=0.1)(
                *in_vmem(sums, message), *others
            )

        other, own = to_column(other, 1), to_column(own, 1)
        current = settled(own_sums, other)
        beside = to_sibling(current)
        packed = coeffs_call(*in_vmem(current, column_basis, column_transfer))
        packed_column = to_column(packed, 1)
        column = settled(other_sums, own, packed, beside)
        crossing, diagonal, send, keep = half_call(
            in_smem(both_places), *in_vmem(mine, theirs, current, beside, column, to_sibling(column))
        )
        crossed, arrived = to_column(crossing, 1), to_sibling(send)
        diagonal = lax.ppermute(diagonal, "loop", [(i, i ^ 3) for i in range(count)])
        self_part = self_call(current, us=0.6)
        far_part = far_call(table, all_coeffs(packed, [packed_column]))
        return call(last_kernel, "last", panels(clusters, BF16), [VMEM_SPEC] * 6, us=0.1)(
            *in_vmem(self_part, far_part, keep, crossed, arrived, diagonal)
        )

    self_part = self_call(current)
    far_part = far_call(table, pieces, starts)

    def finished():
        near = keep_own + arrived_own[:clusters].astype(F32)
        for s in range(1, columns):
            part = slice((s - 1) * clusters, s * clusters)
            partial = (keep[part] + arrived[part].astype(F32)).astype(BF16)
            near = near + to_column(partial, s).astype(F32)
        return (self_part + far_part + near).astype(BF16)

    for step in range(1, ITERS):
        message = call(
            message_kernel, "message", panels(clusters + rows, BF16), [VMEM_SPEC] * 3, us=0.5
        )(*in_vmem(finished(), column_basis, column_transfer))
        messages = gather(message)
        send, send_own, keep, keep_own = near_call(table, messages)
        arrived, arrived_own = to_sibling(send), to_sibling(send_own)
        self_part = self_call(message)
        far_part = far_call(table, messages)
    return finished()


def solution(mesh):
    in_specs = (
        P(("groups", "loop"), "cuts", None),
        P(("groups", "loop"), None, None),
        P(("groups", "loop"), None, None),
        P(("groups", "loop"), None),
        P(("groups", "loop"), None),
        P(("groups", "loop"), None),
        P(("groups", "loop"), None, None),
        P(("groups", "loop"), None, None),
        P(("groups", "loop"), None, None),
        P(("groups", "loop"), None, None),
        P(("groups", "loop"), None, None),
        P(("groups", "loop"), None),
    )
    out_specs = P(("groups", "loop"), "cuts", None)
    return jax.shard_map(
        on_device, mesh=mesh, in_specs=in_specs, out_specs=out_specs, check_vma=False
    )
```

```python
import functools

import jax
import jax.numpy as jnp
from jax import lax
from jax.experimental import pallas as pl
from jax.experimental.pallas import tpu as pltpu
from jax.sharding import PartitionSpec as P

ITERS = 2
F32, BF16 = jnp.float32, jnp.bfloat16
ROWS_BY_ROWS = (((1,), (1,)), ((), ()))
ROWS_BY_COLUMNS = (((1,), (0,)), ((), ()))
VMEM_LIMIT = 8 * 1024 * 1024
FAR_ROW = 8


def dot(a, b, dims):
    return lax.dot_general(a, b, dims, preferred_element_type=F32)


def dot_wide(a, b, dims):
    rows = a.shape[0]
    upper = a.astype(BF16).astype(F32)
    halves = jnp.concatenate([upper, a - upper], axis=0).astype(BF16)
    both = dot(halves, b, dims)
    return both[:rows] + both[rows:]


def lanes_below(vectors, lanes):
    return lax.broadcasted_iota(jnp.int32, (vectors, lanes), 1) < lanes // 2


def load_all(sems, *pairs):
    copies = [pltpu.make_async_copy(x, y, sems.at[i]) for i, (x, y) in enumerate(pairs)]
    for copy in copies:
        copy.start()
    return copies


def parent_coeffs(current, column_basis, column_transfer, packed, first):
    clusters, rank, leaf_size = column_basis.shape
    vectors = current.shape[1]
    parents = clusters // 2
    lower = lanes_below(vectors, 2 * rank)
    leaves = []
    for p in range(parents):
        both = dot(
            current[2 * p : 2 * p + 2].reshape(2 * vectors, leaf_size),
            column_basis[2 * p : 2 * p + 2].reshape(2 * rank, leaf_size),
            ROWS_BY_ROWS,
        )
        leaves.append(jnp.where(lower, both[:vectors], both[vectors:]))
    totals = []
    for p in range(parents):
        transfer = column_transfer[2 * p : 2 * p + 2].reshape(2 * rank, rank)
        totals.append(dot_wide(leaves[p], transfer, ROWS_BY_COLUMNS))
    each = leaf_size // rank
    for p in range(0, parents, each):
        row = jnp.concatenate(totals[p : p + each], axis=-1)
        packed[first + p // each] = row.astype(BF16)


def unpack(packed, first, rows, rank, gathered, slot):
    for r in range(rows):
        row = packed[first + r].astype(F32)
        for k in range(row.shape[1] // (2 * rank)):
            pair = row[:, 2 * rank * k : 2 * rank * (k + 1)]
            lower = lanes_below(*pair.shape)
            turned = pltpu.roll(pair, rank, 1)
            gathered[slot] = jnp.where(lower, pair, turned).astype(BF16)
            gathered[slot + 1] = jnp.where(lower, turned, pair).astype(BF16)
            slot += 2
    return slot


def place_table(columns, clusters, source, target, local, far, values, places):
    me = lax.axis_index("loop")
    my_column = me // 2

    def around(shift):
        return jnp.where(shift < 0, shift + columns, shift)

    def other_core(home):
        return (home ^ me) & 1

    blocks = source.shape[1]
    home = source[...]
    shift = around(my_column - (home >> 1))
    values[0:1, :blocks] = (2 * shift + other_core(home)) * clusters + local[0:1]
    home = target[...]
    shift = around((home >> 1) - my_column)
    values[1:2, :blocks] = ((1 - other_core(home)) * columns + shift) * clusters + local[1:2]
    cluster = far[...]
    parents, far_count = cluster.shape
    home = jnp.zeros_like(cluster)
    for h in range(1, 2 * columns):
        home = home + jnp.where(cluster >= h * parents, 1, 0)
    shift = around(my_column - (home >> 1))
    place = (2 * shift + other_core(home)) * parents + cluster - home * parents
    values[FAR_ROW : FAR_ROW + parents, :far_count] = place
    home = source[...]
    shift = around(my_column - (home >> 1))
    places[0:1, :blocks] = (2 * shift + (home & 1)) * clusters + local[0:1]
    home = target[...]
    shift = around((home >> 1) - my_column)
    places[1:2, :blocks] = (2 * shift + (home & 1)) * clusters + local[1:2]


def first_kernel(
    columns,
    source_home,
    target_home,
    block_local,
    far_source,
    vectors,
    column_basis,
    column_transfer,
    packed,
    current,
    places,
    table,
    basis_held,
    transfer_held,
    source,
    target,
    local,
    far,
    values,
    sems,
):
    copies = load_all(
        sems,
        (source_home, source),
        (target_home, target),
        (block_local, local),
        (far_source, far),
        (vectors, current),
        (column_basis, basis_held),
        (column_transfer, transfer_held),
    )
    for copy in copies[:4]:
        copy.wait()
    place_table(columns, vectors.shape[0], source, target, local, far, values, places)
    placed = pltpu.make_async_copy(values, table, sems.at[7])
    placed.start()
    for copy in copies[4:]:
        copy.wait()
    parent_coeffs(current, basis_held, transfer_held, packed, 0)
    placed.wait()


def coeffs_kernel(current, column_basis, column_transfer, packed):
    parent_coeffs(current, column_basis, column_transfer, packed, 0)


def message_kernel(current, column_basis, column_transfer, message):
    clusters = current.shape[0]
    message[:clusters] = current[...]
    parent_coeffs(current, column_basis, column_transfer, message, clusters)


def self_kernel(current, self_tiles, *others):
    self_part = others[-1]
    for c in range(self_part.shape[0]):
        self_part[c] = dot(current[c], self_tiles[c], ROWS_BY_ROWS)


def turn_kernel(tiles, mine, theirs):
    lanes = mine.shape[2]
    core = lax.axis_index("loop") % 2
    start = pl.multiple_of(core * lanes, lanes)
    other = pl.multiple_of((1 - core) * lanes, lanes)
    for b in range(tiles.shape[0]):
        mine[b] = tiles[b, pl.ds(start, lanes), :].T
        theirs[b] = tiles[b, pl.ds(other, lanes), :].T


def near_kernel(panel_count, packed_count, table, mine, theirs, *refs):
    panels, refs = refs[:panel_count], refs[panel_count:]
    packed = refs[:packed_count]
    send, keep, keep_own, gathered, products, sums = refs[-6:]
    each = gathered.shape[0] // panel_count
    for k, panel in enumerate(panels):
        gathered[k * each : (k + 1) * each] = panel[:each]
    sums[...] = jnp.zeros_like(sums)
    blocks = mine.shape[0]
    for b in range(blocks):
        tile = jnp.concatenate([mine[b], theirs[b]], axis=-1)
        products[b] = dot(gathered[table[0, b]], tile, ROWS_BY_COLUMNS)
    for b in range(blocks):
        sums[table[1, b]] += products[b]
    own, half = keep_own.shape[0], sums.shape[0] // 2
    core = lax.axis_index("loop") % 2

    def in_order(x):
        lanes = x.shape[-1] // 2
        here, beside = x[..., :lanes], x[..., lanes:]
        return jnp.concatenate(
            [jnp.where(core == 0, here, beside), jnp.where(core == 0, beside, here)], axis=-1
        )

    send[half - own : half] = in_order(sums[:own]).astype(BF16)
    for k, coeffs in enumerate(packed):
        rows = coeffs.shape[0]
        send[half + k * rows : half + (k + 1) * rows] = coeffs[...]
    send[: half - own] = in_order(sums[own:half]).astype(BF16)
    keep_own[...] = in_order(sums[half : half + own])
    keep[...] = in_order(sums[half + own :])


def first_self_kernel(
    current, self_tiles, places, places_beside, sent_before, self_part, table, sems
):
    copies = load_all(
        sems,
        (places, table.at[pl.ds(0, FAR_ROW)]),
        (places_beside, table.at[pl.ds(FAR_ROW, FAR_ROW)]),
    )
    self_kernel(current, self_tiles, self_part)
    for copy in copies:
        copy.wait()


def half_kernel(
    table,
    mine,
    beside,
    current,
    current_beside,
    column,
    column_beside,
    across,
    diagonal,
    send,
    keep,
    gathered,
    products,
    sums,
):
    clusters = current.shape[0]
    core = lax.axis_index("loop") % 2

    def at(slot):
        return pl.ds(slot * clusters, clusters)

    gathered[at(core)] = current[...]
    gathered[at(1 - core)] = current_beside[...]
    gathered[at(2 + core)] = column[...]
    gathered[at(3 - core)] = column_beside[...]
    sums[...] = jnp.zeros_like(sums)
    blocks = mine.shape[0]
    for k, tiles in enumerate((mine, beside)):
        for b in range(blocks):
            source = table[k * FAR_ROW, b]
            products[k * blocks + b] = dot(gathered[source], tiles[b], ROWS_BY_COLUMNS)
    for k in range(2):
        for b in range(blocks):
            sums[table[k * FAR_ROW + 1, b]] += products[k * blocks + b]
    across[...] = sums[at(2 + core)].astype(BF16)
    diagonal[...] = sums[at(3 - core)].astype(BF16)
    send[...] = sums[at(1 - core)].astype(BF16)
    keep[...] = sums[at(core)]


def far_products(table, row_transfer, row_basis, coupling, gathered, store):
    vectors, lanes = gathered.shape[1:]
    rank, leaf_size = row_basis.shape[1:]
    parents = coupling.shape[0]
    far_count = coupling.shape[2] // rank
    lower = lanes_below(vectors, lanes)
    parent_outs = []
    for p in range(parents):
        pairs = []
        for f in range(0, far_count, 2):
            first = gathered[table[FAR_ROW + p, f]]
            second = gathered[table[FAR_ROW + p, f + 1]]
            pairs.append(jnp.where(lower, first.astype(F32), second.astype(F32)).astype(BF16))
        parent_outs.append(dot(jnp.concatenate(pairs, axis=-1), coupling[p], ROWS_BY_ROWS))
    leaf_outs = []
    for p in range(parents):
        transfer = jnp.concatenate([row_transfer[2 * p], row_transfer[2 * p + 1]], axis=-1)
        leaf_outs.append(dot_wide(parent_outs[p], transfer, ROWS_BY_COLUMNS))
    for p in range(parents):
        zero = jnp.zeros_like(leaf_outs[p])
        stacked = jnp.concatenate(
            [jnp.where(lower, leaf_outs[p], zero), jnp.where(lower, zero, leaf_outs[p])], axis=0
        ).astype(BF16)
        basis = row_basis[2 * p : 2 * p + 2].reshape(2 * rank, leaf_size)
        both = dot(stacked, basis, ROWS_BY_COLUMNS)
        store(2 * p, both.reshape(2, vectors, leaf_size))


def far_kernel(starts, rows, table, row_transfer, row_basis, coupling, *refs):
    messages, (far_part, gathered) = refs[: len(starts)], refs[-2:]
    slot = 0
    for message, start in zip(messages, starts):
        slot = unpack(message, start, rows, row_basis.shape[1], gathered, slot)

    def store(c, both):
        far_part[c : c + 2] = both

    far_products(table, row_transfer, row_basis, coupling, gathered, store)


def other_kernel(keep, arrived, message, sums):
    other = keep[...] + arrived[: keep.shape[0]].astype(F32)
    sums[...] = other
    message[...] = other.astype(BF16)


def own_kernel(keep, arrived, self_part, far_part, sent_before, message, sums):
    own_rows = pl.ds(keep.shape[0], keep.shape[0])
    near = keep[...] + arrived[own_rows].astype(F32)
    own = near + self_part[...] + far_part[...]
    sums[...] = own
    message[...] = own.astype(BF16)


def settle_kernel(sums, message, *others):
    current = others[-1]
    current[...] = (sums[...] + message[...].astype(F32)).astype(BF16)


def last_kernel(self_part, far_part, keep, crossed, arrived, diagonal, product):
    core = lax.axis_index("loop") % 2
    here = keep[...] + crossed[...].astype(F32)
    beside = arrived[...].astype(F32) + diagonal[...].astype(F32)
    near = jnp.concatenate(
        [jnp.where(core == 0, here, beside), jnp.where(core == 0, beside, here)], axis=-1
    )
    product[...] = (self_part[...] + far_part[...] + near).astype(BF16)


def tie_kernel(*refs):
    pass


def in_vmem(*arrays):
    return [pltpu.with_memory_space_constraint(a, pltpu.VMEM) for a in arrays]


def in_hbm(*arrays):
    return [pltpu.with_memory_space_constraint(a, pltpu.HBM) for a in arrays]


def in_smem(array):
    return pltpu.with_memory_space_constraint(array, pltpu.SMEM)


VMEM_SPEC = pl.BlockSpec(memory_space=pltpu.VMEM)
HBM_SPEC = pl.BlockSpec(memory_space=pltpu.HBM)
ANY_SPEC = pl.BlockSpec(memory_space=pl.ANY)
SMEM_SPEC = pl.BlockSpec(memory_space=pltpu.SMEM)


def call(kernel, name, out_shape, in_specs, scratch_shapes=(), out_specs=None, us=1.0):
    return pl.pallas_call(
        kernel,
        name=name,
        out_shape=out_shape,
        in_specs=in_specs,
        out_specs=jax.tree.map(lambda _: VMEM_SPEC, out_shape) if out_specs is None else out_specs,
        scratch_shapes=scratch_shapes,
        compiler_params=pltpu.CompilerParams(vmem_limit_bytes=VMEM_LIMIT),
        cost_estimate=pl.CostEstimate(
            flops=int(us * 1.0e9), bytes_accessed=0, transcendentals=0
        ),
    )


def tie(x, *others, us=0.0):
    return pl.pallas_call(
        tie_kernel,
        name="tie",
        out_shape=pltpu.VMEM(x.shape, x.dtype),
        in_specs=[VMEM_SPEC] + [ANY_SPEC] * len(others),
        out_specs=VMEM_SPEC,
        input_output_aliases={0: 0},
        compiler_params=pltpu.CompilerParams(vmem_limit_bytes=VMEM_LIMIT),
        cost_estimate=pl.CostEstimate(
            flops=int(us * 1.0e9), bytes_accessed=0, transcendentals=0
        ),
    )(*in_vmem(x), *others)


def on_device(
    vectors,
    near_tiles,
    self_tiles,
    source_home,
    target_home,
    block_local,
    column_basis,
    row_basis,
    column_transfer,
    row_transfer,
    coupling,
    far_source,
):
    clusters, vector_count, leaf_size = vectors.shape
    blocks = near_tiles.shape[0]
    rank = column_basis.shape[1]
    parents, far_count = far_source.shape
    count = lax.axis_size("loop")
    columns = count // 2
    sibling = [(i, i ^ 1) for i in range(count)]

    def to_sibling(x):
        return lax.ppermute(x, "loop", sibling)

    def to_column(x, shift):
        return lax.ppermute(x, "loop", [(i, (i + 2 * shift) % count) for i in range(count)])

    def across(x):
        return [to_column(x, shift) for shift in range(1, columns)]

    def panels(number, dtype, width=leaf_size):
        return jax.ShapeDtypeStruct((number, vector_count, width), dtype)

    def scratch(number, dtype, width=leaf_size):
        return pltpu.VMEM((number, vector_count, width), dtype)

    rows = parents * rank // leaf_size
    raw = (source_home.T, target_home.T, block_local.T, far_source)
    table_shape = (FAR_ROW + parents, 128)
    first_call = call(
        functools.partial(first_kernel, columns),
        "first",
        (
            panels(rows, BF16),
            pltpu.VMEM(vectors.shape, BF16),
            pltpu.VMEM((FAR_ROW, 128), jnp.int32),
            pltpu.SMEM(table_shape, jnp.int32),
        ),
        [HBM_SPEC] * 7,
        [pltpu.VMEM(x.shape, x.dtype) for x in (column_basis, column_transfer, *raw)]
        + [pltpu.VMEM(table_shape, jnp.int32), pltpu.SemaphoreType.DMA((8,))],
        out_specs=(VMEM_SPEC, VMEM_SPEC, VMEM_SPEC, SMEM_SPEC),
        us=10.0,
    )
    half_tiles = pltpu.VMEM((blocks, leaf_size, leaf_size // 2), BF16)
    turn_call = call(turn_kernel, "turn", (half_tiles, half_tiles), [VMEM_SPEC], us=2.5)
    coeffs_call = call(coeffs_kernel, "coeffs", panels(rows, BF16), [VMEM_SPEC] * 3, us=0.5)
    def self_call(current, *others, us=0.6):
        specs = [VMEM_SPEC] * 2 + [ANY_SPEC] * len(others)
        return call(self_kernel, "self", panels(clusters, F32), specs, us=us)(
            *in_vmem(current, self_tiles), *others
        )

    def near_call(table, given, packed=()):
        return call(
            functools.partial(near_kernel, len(given), len(packed)),
            "near",
            (
                panels(columns * clusters + len(packed) * rows, BF16),
                panels((columns - 1) * clusters, F32),
                panels(clusters, F32),
            ),
            [SMEM_SPEC] + [VMEM_SPEC] * (2 + len(given) + len(packed)),
            [
                scratch(count * clusters, BF16),
                scratch(blocks, F32),
                scratch(count * clusters, F32),
            ],
            us=1.0,
        )(in_smem(table), *in_vmem(mine, theirs, *given, *packed))

    half_size = leaf_size // 2
    first_self_call = call(
        first_self_kernel,
        "first_self",
        (panels(clusters, F32), pltpu.SMEM((2 * FAR_ROW, 128), jnp.int32)),
        [VMEM_SPEC] * 4 + [ANY_SPEC],
        [pltpu.SemaphoreType.DMA((2,))],
        out_specs=(VMEM_SPEC, SMEM_SPEC),
        us=0.6,
    )
    half_call = call(
        half_kernel,
        "half",
        (*(panels(clusters, BF16, half_size),) * 3, panels(clusters, F32, half_size)),
        [SMEM_SPEC] + [VMEM_SPEC] * 6,
        [
            scratch(count * clusters, BF16),
            scratch(2 * blocks, F32, half_size),
            scratch(count * clusters, F32, half_size),
        ],
        us=1.0,
    )

    gathered_coeffs = scratch(count * parents, BF16, 2 * rank)

    def far_call(table, messages, starts=None):
        if starts is None:
            starts = [x.shape[0] - rows for x in messages]
        return call(
            functools.partial(far_kernel, tuple(starts), rows),
            "far",
            panels(clusters, F32),
            [SMEM_SPEC] + [VMEM_SPEC] * (3 + len(messages)),
            [gathered_coeffs],
            us=0.5,
        )(in_smem(table), *in_vmem(row_transfer, row_basis, coupling, *messages))

    def gather(message, *others):
        gathered = [message, to_sibling(message)]
        for x in across(message):
            gathered += [x, to_sibling(tie(x, *others) if others else x)]
        return gathered

    def all_coeffs(packed, crossed):
        beside = to_sibling(jnp.concatenate([packed, *crossed]))
        pieces = []
        for k, piece in enumerate([packed, *crossed]):
            pieces += [piece, beside[k * rows : (k + 1) * rows]]
        return pieces

    crossed = across(vectors)
    packed, current, places, table = first_call(*in_hbm(*raw, vectors, column_basis, column_transfer))
    places_beside = to_sibling(places)
    given = [current, to_sibling(current)]
    for x in crossed:
        given += [x, to_sibling(tie(x, packed, places_beside))]
    crossed = across(packed)
    mine, theirs = turn_call(*in_vmem(near_tiles))
    send, keep, keep_own = near_call(table, given, [packed, *crossed])
    arrived = to_sibling(send)
    pieces, starts = [], []
    for k, piece in enumerate([packed, *crossed]):
        pieces += [piece, arrived]
        starts += [0, columns * clusters + k * rows]

    if columns == 2 and ITERS == 2:
        both_out = (panels(clusters, BF16), panels(clusters, F32))
        other, other_sums = call(other_kernel, "other", both_out, [VMEM_SPEC] * 2, us=0.1)(
            *in_vmem(keep, arrived)
        )
        far_part = far_call(table, pieces, starts)
        self_part, both_places = first_self_call(
            *in_vmem(current, self_tiles, places, places_beside), other
        )
        theirs = to_sibling(tie(theirs, other, places_beside))
        own, own_sums = call(
            own_kernel, "own", both_out, [VMEM_SPEC] * 4 + [ANY_SPEC], us=0.1
        )(*in_vmem(keep_own, arrived, self_part, far_part), other)

        def settled(sums, message, *others):
            specs = [VMEM_SPEC] * 2 + [ANY_SPEC] * len(others)
            return call(settle_kernel, "settle", panels(clusters, BF16), specs, us=0.1)(
                *in_vmem(sums, message), *others
            )

        other, own = to_column(other, 1), to_column(own, 1)
        current = settled(own_sums, other)
        beside = to_sibling(current)
        packed = coeffs_call(*in_vmem(current, column_basis, column_transfer))
        packed_column = to_column(packed, 1)
        column = settled(other_sums, own, packed, beside)
        crossing, diagonal, send, keep = half_call(
            in_smem(both_places), *in_vmem(mine, theirs, current, beside, column, to_sibling(column))
        )
        crossed, arrived = to_column(crossing, 1), to_sibling(send)
        diagonal = lax.ppermute(diagonal, "loop", [(i, i ^ 3) for i in range(count)])
        self_part = self_call(current, us=0.6)
        far_part = far_call(table, all_coeffs(packed, [packed_column]))
        return call(last_kernel, "last", panels(clusters, BF16), [VMEM_SPEC] * 6, us=0.1)(
            *in_vmem(self_part, far_part, keep, crossed, arrived, diagonal)
        )

    self_part = self_call(current)
    far_part = far_call(table, pieces, starts)

    def finished():
        near = keep_own + arrived[(columns - 1) * clusters : columns * clusters].astype(F32)
        for s in range(1, columns):
            part = slice((s - 1) * clusters, s * clusters)
            partial = (keep[part] + arrived[part].astype(F32)).astype(BF16)
            near = near + to_column(partial, s).astype(F32)
        return (self_part + far_part + near).astype(BF16)

    for step in range(1, ITERS):
        message = call(
            message_kernel, "message", panels(clusters + rows, BF16), [VMEM_SPEC] * 3, us=0.5
        )(*in_vmem(finished(), column_basis, column_transfer))
        messages = gather(message)
        send, keep, keep_own = near_call(table, messages)
        arrived = to_sibling(send)
        self_part = self_call(message)
        far_part = far_call(table, messages)
    return finished()


def solution(mesh):
    in_specs = (
        P(("groups", "loop"), "cuts", None),
        P(("groups", "loop"), None, None),
        P(("groups", "loop"), None, None),
        P(("groups", "loop"), None),
        P(("groups", "loop"), None),
        P(("groups", "loop"), None),
        P(("groups", "loop"), None, None),
        P(("groups", "loop"), None, None),
        P(("groups", "loop"), None, None),
        P(("groups", "loop"), None, None),
        P(("groups", "loop"), None, None),
        P(("groups", "loop"), None),
    )
    out_specs = P(("groups", "loop"), "cuts", None)
    return jax.shard_map(
        on_device, mesh=mesh, in_specs=in_specs, out_specs=out_specs, check_vma=False
    )
```

```python
import functools

import jax
import jax.numpy as jnp
from jax import lax
from jax.experimental import pallas as pl
from jax.experimental.pallas import tpu as pltpu
from jax.sharding import PartitionSpec as P

ITERS = 2
F32, BF16 = jnp.float32, jnp.bfloat16
ROWS_BY_ROWS = (((1,), (1,)), ((), ()))
ROWS_BY_COLUMNS = (((1,), (0,)), ((), ()))
VMEM_LIMIT = 8 * 1024 * 1024
FAR_ROW = 8


def dot(a, b, dims):
    return lax.dot_general(a, b, dims, preferred_element_type=F32)


def dot_wide(a, b, dims):
    rows = a.shape[0]
    upper = a.astype(BF16).astype(F32)
    halves = jnp.concatenate([upper, a - upper], axis=0).astype(BF16)
    both = dot(halves, b, dims)
    return both[:rows] + both[rows:]


def lanes_below(vectors, lanes):
    return lax.broadcasted_iota(jnp.int32, (vectors, lanes), 1) < lanes // 2


def load_all(sems, *pairs):
    copies = [pltpu.make_async_copy(x, y, sems.at[i]) for i, (x, y) in enumerate(pairs)]
    for copy in copies:
        copy.start()
    return copies


def parent_coeffs(current, column_basis, column_transfer, packed, first):
    clusters, rank, leaf_size = column_basis.shape
    vectors = current.shape[1]
    parents = clusters // 2
    lower = lanes_below(vectors, 2 * rank)
    leaves = []
    for p in range(parents):
        both = dot(
            current[2 * p : 2 * p + 2].reshape(2 * vectors, leaf_size),
            column_basis[2 * p : 2 * p + 2].reshape(2 * rank, leaf_size),
            ROWS_BY_ROWS,
        )
        leaves.append(jnp.where(lower, both[:vectors], both[vectors:]))
    totals = []
    for p in range(parents):
        transfer = column_transfer[2 * p : 2 * p + 2].reshape(2 * rank, rank)
        totals.append(dot_wide(leaves[p], transfer, ROWS_BY_COLUMNS))
    each = leaf_size // rank
    for p in range(0, parents, each):
        row = jnp.concatenate(totals[p : p + each], axis=-1)
        packed[first + p // each] = row.astype(BF16)


def unpack(packed, first, rows, rank, gathered, slot):
    for r in range(rows):
        row = packed[first + r].astype(F32)
        for k in range(row.shape[1] // (2 * rank)):
            pair = row[:, 2 * rank * k : 2 * rank * (k + 1)]
            lower = lanes_below(*pair.shape)
            turned = pltpu.roll(pair, rank, 1)
            gathered[slot] = jnp.where(lower, pair, turned).astype(BF16)
            gathered[slot + 1] = jnp.where(lower, turned, pair).astype(BF16)
            slot += 2
    return slot


def place_table(columns, clusters, source, target, local, far, values, places):
    me = lax.axis_index("loop")
    my_column = me // 2

    def around(shift):
        return jnp.where(shift < 0, shift + columns, shift)

    def other_core(home):
        return (home ^ me) & 1

    blocks = source.shape[1]
    home = source[...]
    shift = around(my_column - (home >> 1))
    values[0:1, :blocks] = (2 * shift + other_core(home)) * clusters + local[0:1]
    home = target[...]
    shift = around((home >> 1) - my_column)
    values[1:2, :blocks] = ((1 - other_core(home)) * columns + shift) * clusters + local[1:2]
    cluster = far[...]
    parents, far_count = cluster.shape
    home = jnp.zeros_like(cluster)
    for h in range(1, 2 * columns):
        home = home + jnp.where(cluster >= h * parents, 1, 0)
    shift = around(my_column - (home >> 1))
    place = (2 * shift + other_core(home)) * parents + cluster - home * parents
    values[FAR_ROW : FAR_ROW + parents, :far_count] = place
    home = source[...]
    shift = around(my_column - (home >> 1))
    places[0:1, :blocks] = (2 * shift + (home & 1)) * clusters + local[0:1]
    home = target[...]
    shift = around((home >> 1) - my_column)
    places[1:2, :blocks] = (2 * shift + (home & 1)) * clusters + local[1:2]


def first_kernel(
    columns,
    source_home,
    target_home,
    block_local,
    far_source,
    vectors,
    column_basis,
    column_transfer,
    packed,
    current,
    places,
    table,
    basis_held,
    transfer_held,
    source,
    target,
    local,
    far,
    values,
    sems,
):
    copies = load_all(
        sems,
        (column_basis, basis_held),
        (vectors, current),
        (column_transfer, transfer_held),
        (source_home, source),
        (target_home, target),
        (block_local, local),
        (far_source, far),
    )
    for copy in copies[3:]:
        copy.wait()
    place_table(columns, vectors.shape[0], source, target, local, far, values, places)
    placed = pltpu.make_async_copy(values, table, sems.at[7])
    placed.start()
    for copy in copies[:3]:
        copy.wait()
    parent_coeffs(current, basis_held, transfer_held, packed, 0)
    placed.wait()


def coeffs_kernel(current, column_basis, column_transfer, packed):
    parent_coeffs(current, column_basis, column_transfer, packed, 0)


def message_kernel(current, column_basis, column_transfer, message):
    clusters = current.shape[0]
    message[:clusters] = current[...]
    parent_coeffs(current, column_basis, column_transfer, message, clusters)


def self_kernel(current, self_tiles, *others):
    self_part = others[-1]
    for c in range(self_part.shape[0]):
        self_part[c] = dot(current[c], self_tiles[c], ROWS_BY_ROWS)


def turn_kernel(tiles, mine, theirs):
    lanes = mine.shape[2]
    core = lax.axis_index("loop") % 2
    start = pl.multiple_of(core * lanes, lanes)
    other = pl.multiple_of((1 - core) * lanes, lanes)
    for b in range(tiles.shape[0]):
        mine[b] = tiles[b, pl.ds(start, lanes), :].T
        theirs[b] = tiles[b, pl.ds(other, lanes), :].T


def near_kernel(panel_count, packed_count, table, mine, theirs, *refs):
    panels, refs = refs[:panel_count], refs[panel_count:]
    packed = refs[:packed_count]
    send, keep, keep_own, gathered, products, sums = refs[-6:]
    each = gathered.shape[0] // panel_count
    for k, panel in enumerate(panels):
        gathered[k * each : (k + 1) * each] = panel[:each]
    sums[...] = jnp.zeros_like(sums)
    blocks = mine.shape[0]
    for b in range(blocks):
        tile = jnp.concatenate([mine[b], theirs[b]], axis=-1)
        products[b] = dot(gathered[table[0, b]], tile, ROWS_BY_COLUMNS)
    for b in range(blocks):
        sums[table[1, b]] += products[b]
    own, half = keep_own.shape[0], sums.shape[0] // 2
    core = lax.axis_index("loop") % 2

    def in_order(x):
        lanes = x.shape[-1] // 2
        here, beside = x[..., :lanes], x[..., lanes:]
        return jnp.concatenate(
            [jnp.where(core == 0, here, beside), jnp.where(core == 0, beside, here)], axis=-1
        )

    send[half - own : half] = in_order(sums[:own]).astype(BF16)
    for k, coeffs in enumerate(packed):
        rows = coeffs.shape[0]
        send[half + k * rows : half + (k + 1) * rows] = coeffs[...]
    send[: half - own] = in_order(sums[own:half]).astype(BF16)
    keep_own[...] = in_order(sums[half : half + own])
    keep[...] = in_order(sums[half + own :])


def first_self_kernel(
    current, self_tiles, places, places_beside, sent_before, self_part, table, sems
):
    copies = load_all(
        sems,
        (places, table.at[pl.ds(0, FAR_ROW)]),
        (places_beside, table.at[pl.ds(FAR_ROW, FAR_ROW)]),
    )
    self_kernel(current, self_tiles, self_part)
    for copy in copies:
        copy.wait()


def half_kernel(
    table,
    mine,
    beside,
    current,
    current_beside,
    column,
    column_beside,
    across,
    diagonal,
    send,
    keep,
    gathered,
    products,
    sums,
):
    clusters = current.shape[0]
    core = lax.axis_index("loop") % 2

    def at(slot):
        return pl.ds(slot * clusters, clusters)

    gathered[at(core)] = current[...]
    gathered[at(1 - core)] = current_beside[...]
    gathered[at(2 + core)] = column[...]
    gathered[at(3 - core)] = column_beside[...]
    sums[...] = jnp.zeros_like(sums)
    blocks = mine.shape[0]
    for k, tiles in enumerate((mine, beside)):
        for b in range(blocks):
            source = table[k * FAR_ROW, b]
            products[k * blocks + b] = dot(gathered[source], tiles[b], ROWS_BY_COLUMNS)
    for k in range(2):
        for b in range(blocks):
            sums[table[k * FAR_ROW + 1, b]] += products[k * blocks + b]
    across[...] = sums[at(2 + core)].astype(BF16)
    diagonal[...] = sums[at(3 - core)].astype(BF16)
    send[...] = sums[at(1 - core)].astype(BF16)
    keep[...] = sums[at(core)]


def far_products(table, row_transfer, row_basis, coupling, gathered, store):
    vectors, lanes = gathered.shape[1:]
    rank, leaf_size = row_basis.shape[1:]
    parents = coupling.shape[0]
    far_count = coupling.shape[2] // rank
    lower = lanes_below(vectors, lanes)
    parent_outs = []
    for p in range(parents):
        pairs = []
        for f in range(0, far_count, 2):
            first = gathered[table[FAR_ROW + p, f]]
            second = gathered[table[FAR_ROW + p, f + 1]]
            pairs.append(jnp.where(lower, first.astype(F32), second.astype(F32)).astype(BF16))
        parent_outs.append(dot(jnp.concatenate(pairs, axis=-1), coupling[p], ROWS_BY_ROWS))
    leaf_outs = []
    for p in range(parents):
        transfer = jnp.concatenate([row_transfer[2 * p], row_transfer[2 * p + 1]], axis=-1)
        leaf_outs.append(dot_wide(parent_outs[p], transfer, ROWS_BY_COLUMNS))
    for p in range(parents):
        zero = jnp.zeros_like(leaf_outs[p])
        stacked = jnp.concatenate(
            [jnp.where(lower, leaf_outs[p], zero), jnp.where(lower, zero, leaf_outs[p])], axis=0
        ).astype(BF16)
        basis = row_basis[2 * p : 2 * p + 2].reshape(2 * rank, leaf_size)
        both = dot(stacked, basis, ROWS_BY_COLUMNS)
        store(2 * p, both.reshape(2, vectors, leaf_size))


def far_kernel(starts, rows, table, row_transfer, row_basis, coupling, *refs):
    messages, (far_part, gathered) = refs[: len(starts)], refs[-2:]
    slot = 0
    for message, start in zip(messages, starts):
        slot = unpack(message, start, rows, row_basis.shape[1], gathered, slot)

    def store(c, both):
        far_part[c : c + 2] = both

    far_products(table, row_transfer, row_basis, coupling, gathered, store)


def other_kernel(keep, arrived, message, sums):
    other = keep[...] + arrived[: keep.shape[0]].astype(F32)
    sums[...] = other
    message[...] = other.astype(BF16)


def own_kernel(keep, arrived, self_part, far_part, sent_before, message, sums):
    own_rows = pl.ds(keep.shape[0], keep.shape[0])
    near = keep[...] + arrived[own_rows].astype(F32)
    own = near + self_part[...] + far_part[...]
    sums[...] = own
    message[...] = own.astype(BF16)


def settle_kernel(sums, message, *others):
    current = others[-1]
    current[...] = (sums[...] + message[...].astype(F32)).astype(BF16)


def last_kernel(self_part, far_part, keep, crossed, arrived, diagonal, product):
    core = lax.axis_index("loop") % 2
    here = keep[...] + crossed[...].astype(F32)
    beside = arrived[...].astype(F32) + diagonal[...].astype(F32)
    near = jnp.concatenate(
        [jnp.where(core == 0, here, beside), jnp.where(core == 0, beside, here)], axis=-1
    )
    product[...] = (self_part[...] + far_part[...] + near).astype(BF16)


def tie_kernel(*refs):
    pass


def in_vmem(*arrays):
    return [pltpu.with_memory_space_constraint(a, pltpu.VMEM) for a in arrays]


def in_hbm(*arrays):
    return [pltpu.with_memory_space_constraint(a, pltpu.HBM) for a in arrays]


def in_smem(array):
    return pltpu.with_memory_space_constraint(array, pltpu.SMEM)


VMEM_SPEC = pl.BlockSpec(memory_space=pltpu.VMEM)
HBM_SPEC = pl.BlockSpec(memory_space=pltpu.HBM)
ANY_SPEC = pl.BlockSpec(memory_space=pl.ANY)
SMEM_SPEC = pl.BlockSpec(memory_space=pltpu.SMEM)


def call(kernel, name, out_shape, in_specs, scratch_shapes=(), out_specs=None, us=1.0):
    return pl.pallas_call(
        kernel,
        name=name,
        out_shape=out_shape,
        in_specs=in_specs,
        out_specs=jax.tree.map(lambda _: VMEM_SPEC, out_shape) if out_specs is None else out_specs,
        scratch_shapes=scratch_shapes,
        compiler_params=pltpu.CompilerParams(vmem_limit_bytes=VMEM_LIMIT),
        cost_estimate=pl.CostEstimate(
            flops=int(us * 1.0e9), bytes_accessed=0, transcendentals=0
        ),
    )


def tie(x, *others, us=0.0):
    return pl.pallas_call(
        tie_kernel,
        name="tie",
        out_shape=pltpu.VMEM(x.shape, x.dtype),
        in_specs=[VMEM_SPEC] + [ANY_SPEC] * len(others),
        out_specs=VMEM_SPEC,
        input_output_aliases={0: 0},
        compiler_params=pltpu.CompilerParams(vmem_limit_bytes=VMEM_LIMIT),
        cost_estimate=pl.CostEstimate(
            flops=int(us * 1.0e9), bytes_accessed=0, transcendentals=0
        ),
    )(*in_vmem(x), *others)


def on_device(
    vectors,
    near_tiles,
    self_tiles,
    source_home,
    target_home,
    block_local,
    column_basis,
    row_basis,
    column_transfer,
    row_transfer,
    coupling,
    far_source,
):
    clusters, vector_count, leaf_size = vectors.shape
    blocks = near_tiles.shape[0]
    rank = column_basis.shape[1]
    parents, far_count = far_source.shape
    count = lax.axis_size("loop")
    columns = count // 2
    sibling = [(i, i ^ 1) for i in range(count)]

    def to_sibling(x):
        return lax.ppermute(x, "loop", sibling)

    def to_column(x, shift):
        return lax.ppermute(x, "loop", [(i, (i + 2 * shift) % count) for i in range(count)])

    def across(x):
        return [to_column(x, shift) for shift in range(1, columns)]

    def panels(number, dtype, width=leaf_size):
        return jax.ShapeDtypeStruct((number, vector_count, width), dtype)

    def scratch(number, dtype, width=leaf_size):
        return pltpu.VMEM((number, vector_count, width), dtype)

    rows = parents * rank // leaf_size
    raw = (source_home.T, target_home.T, block_local.T, far_source)
    table_shape = (FAR_ROW + parents, 128)
    first_call = call(
        functools.partial(first_kernel, columns),
        "first",
        (
            panels(rows, BF16),
            pltpu.VMEM(vectors.shape, BF16),
            pltpu.VMEM((FAR_ROW, 128), jnp.int32),
            pltpu.SMEM(table_shape, jnp.int32),
        ),
        [HBM_SPEC] * 7,
        [pltpu.VMEM(x.shape, x.dtype) for x in (column_basis, column_transfer, *raw)]
        + [pltpu.VMEM(table_shape, jnp.int32), pltpu.SemaphoreType.DMA((8,))],
        out_specs=(VMEM_SPEC, VMEM_SPEC, VMEM_SPEC, SMEM_SPEC),
        us=10.0,
    )
    half_tiles = pltpu.VMEM((blocks, leaf_size, leaf_size // 2), BF16)
    turn_call = call(turn_kernel, "turn", (half_tiles, half_tiles), [VMEM_SPEC], us=2.5)
    coeffs_call = call(coeffs_kernel, "coeffs", panels(rows, BF16), [VMEM_SPEC] * 3, us=0.5)
    def self_call(current, *others, us=0.6):
        specs = [VMEM_SPEC] * 2 + [ANY_SPEC] * len(others)
        return call(self_kernel, "self", panels(clusters, F32), specs, us=us)(
            *in_vmem(current, self_tiles), *others
        )

    def near_call(table, given, packed=()):
        return call(
            functools.partial(near_kernel, len(given), len(packed)),
            "near",
            (
                panels(columns * clusters + len(packed) * rows, BF16),
                panels((columns - 1) * clusters, F32),
                panels(clusters, F32),
            ),
            [SMEM_SPEC] + [VMEM_SPEC] * (2 + len(given) + len(packed)),
            [
                scratch(count * clusters, BF16),
                scratch(blocks, F32),
                scratch(count * clusters, F32),
            ],
            us=1.0,
        )(in_smem(table), *in_vmem(mine, theirs, *given, *packed))

    half_size = leaf_size // 2
    first_self_call = call(
        first_self_kernel,
        "first_self",
        (panels(clusters, F32), pltpu.SMEM((2 * FAR_ROW, 128), jnp.int32)),
        [VMEM_SPEC] * 4 + [ANY_SPEC],
        [pltpu.SemaphoreType.DMA((2,))],
        out_specs=(VMEM_SPEC, SMEM_SPEC),
        us=0.6,
    )
    half_call = call(
        half_kernel,
        "half",
        (*(panels(clusters, BF16, half_size),) * 3, panels(clusters, F32, half_size)),
        [SMEM_SPEC] + [VMEM_SPEC] * 6,
        [
            scratch(count * clusters, BF16),
            scratch(2 * blocks, F32, half_size),
            scratch(count * clusters, F32, half_size),
        ],
        us=1.0,
    )

    gathered_coeffs = scratch(count * parents, BF16, 2 * rank)

    def far_call(table, messages, starts=None):
        if starts is None:
            starts = [x.shape[0] - rows for x in messages]
        return call(
            functools.partial(far_kernel, tuple(starts), rows),
            "far",
            panels(clusters, F32),
            [SMEM_SPEC] + [VMEM_SPEC] * (3 + len(messages)),
            [gathered_coeffs],
            us=0.5,
        )(in_smem(table), *in_vmem(row_transfer, row_basis, coupling, *messages))

    def gather(message, *others):
        gathered = [message, to_sibling(message)]
        for x in across(message):
            gathered += [x, to_sibling(tie(x, *others) if others else x)]
        return gathered

    def all_coeffs(packed, crossed):
        beside = to_sibling(jnp.concatenate([packed, *crossed]))
        pieces = []
        for k, piece in enumerate([packed, *crossed]):
            pieces += [piece, beside[k * rows : (k + 1) * rows]]
        return pieces

    crossed = across(vectors)
    packed, current, places, table = first_call(*in_hbm(*raw, vectors, column_basis, column_transfer))
    places_beside = to_sibling(places)
    given = [current, to_sibling(current)]
    for x in crossed:
        given += [x, to_sibling(tie(x, packed, places_beside))]
    crossed = across(packed)
    mine, theirs = turn_call(*in_vmem(near_tiles))
    send, keep, keep_own = near_call(table, given, [packed, *crossed])
    arrived = to_sibling(send)
    pieces, starts = [], []
    for k, piece in enumerate([packed, *crossed]):
        pieces += [piece, arrived]
        starts += [0, columns * clusters + k * rows]

    if columns == 2 and ITERS == 2:
        both_out = (panels(clusters, BF16), panels(clusters, F32))
        other, other_sums = call(other_kernel, "other", both_out, [VMEM_SPEC] * 2, us=0.1)(
            *in_vmem(keep, arrived)
        )
        far_part = far_call(table, pieces, starts)
        self_part, both_places = first_self_call(
            *in_vmem(current, self_tiles, places, places_beside), other
        )
        theirs = to_sibling(tie(theirs, other, places_beside))
        own, own_sums = call(
            own_kernel, "own", both_out, [VMEM_SPEC] * 4 + [ANY_SPEC], us=0.1
        )(*in_vmem(keep_own, arrived, self_part, far_part), other)

        def settled(sums, message, *others):
            specs = [VMEM_SPEC] * 2 + [ANY_SPEC] * len(others)
            return call(settle_kernel, "settle", panels(clusters, BF16), specs, us=0.1)(
                *in_vmem(sums, message), *others
            )

        other, own = to_column(other, 1), to_column(own, 1)
        current = settled(own_sums, other)
        beside = to_sibling(current)
        packed = coeffs_call(*in_vmem(current, column_basis, column_transfer))
        packed_column = to_column(packed, 1)
        column = settled(other_sums, own, packed, beside)
        crossing, diagonal, send, keep = half_call(
            in_smem(both_places), *in_vmem(mine, theirs, current, beside, column, to_sibling(column))
        )
        crossed, arrived = to_column(crossing, 1), to_sibling(send)
        diagonal = lax.ppermute(diagonal, "loop", [(i, i ^ 3) for i in range(count)])
        self_part = self_call(current, us=0.6)
        far_part = far_call(table, all_coeffs(packed, [packed_column]))
        return call(last_kernel, "last", panels(clusters, BF16), [VMEM_SPEC] * 6, us=0.1)(
            *in_vmem(self_part, far_part, keep, crossed, arrived, diagonal)
        )

    self_part = self_call(current)
    far_part = far_call(table, pieces, starts)

    def finished():
        near = keep_own + arrived[(columns - 1) * clusters : columns * clusters].astype(F32)
        for s in range(1, columns):
            part = slice((s - 1) * clusters, s * clusters)
            partial = (keep[part] + arrived[part].astype(F32)).astype(BF16)
            near = near + to_column(partial, s).astype(F32)
        return (self_part + far_part + near).astype(BF16)

    for step in range(1, ITERS):
        message = call(
            message_kernel, "message", panels(clusters + rows, BF16), [VMEM_SPEC] * 3, us=0.5
        )(*in_vmem(finished(), column_basis, column_transfer))
        messages = gather(message)
        send, keep, keep_own = near_call(table, messages)
        arrived = to_sibling(send)
        self_part = self_call(message)
        far_part = far_call(table, messages)
    return finished()


def solution(mesh):
    in_specs = (
        P(("groups", "loop"), "cuts", None),
        P(("groups", "loop"), None, None),
        P(("groups", "loop"), None, None),
        P(("groups", "loop"), None),
        P(("groups", "loop"), None),
        P(("groups", "loop"), None),
        P(("groups", "loop"), None, None),
        P(("groups", "loop"), None, None),
        P(("groups", "loop"), None, None),
        P(("groups", "loop"), None, None),
        P(("groups", "loop"), None, None),
        P(("groups", "loop"), None),
    )
    out_specs = P(("groups", "loop"), "cuts", None)
    return jax.shard_map(
        on_device, mesh=mesh, in_specs=in_specs, out_specs=out_specs, check_vma=False
    )
```
